32 devices in a mesh: grp: 2 (over x), slc: 16 (over z, y, core).
Axes of the slice: x: 2, y: 2, z: 4, core: 2. Of those that a mesh axis runs over, the one named last changes fastest.
Arguments:
- kspace: bfloat16 [4, 32, 16, 16384], P('grp', None, None, 'slc'), parts along dimension 0, may hold values from -6 to 6
- coil_maps: bfloat16 [4, 32, 16, 128, 128], P('grp', 'slc'), parts along dimension 0, may hold values from -1 to 1, as said below
- sample_mask: int32 [64, 16, 128], P('grp'), parts along dimension 0, may hold values 0 or 1
- tap_order: int32 [27], replicated, may hold values from 0 to 26, each once
- first_kernel: bfloat16 [27, 2, 64], replicated, may hold values from -0.875 to 0.875
- first_bias: float32 [64], replicated, may hold values from -2 to 2
- second_kernel: bfloat16 [27, 64, 2], replicated, may hold values from -0.15625 to 0.15625
- second_bias: float32 [2], replicated, may hold values from -2 to 2
Outputs:
- estimate: float32 [4, 32, 128, 128], P('grp', 'slc'), parts along dimension 0
- dual_var: float32 [4, 32, 128, 128], P('grp', 'slc'), parts along dimension 0
The draws below stay inside these ranges and needn't reach their ends.
There are 2 independent parts, one for each index of `grp`. The reference program is written for one: setup_inputs(seed, part) draws one part's arguments, and reference() takes and returns one part's arrays. A program takes and returns all parts, laid end to end along the dimension named above; an argument that names none is the same for every part. Nothing has to cross between parts.
Inputs may be any that keep to these rules, and one draw needn't show every extreme that they name: `coil_maps`: at every cell the squared real and imaginary parts of the maps summed over the 16 coils make one, up to rounding. `tap_order`: each tap index appears exactly once.
All inputs are finite; a program needn't handle non-finite values.
Results may differ from the reference program's by a relative error of at most 0.014.
Values may be sent and summed in bfloat16 or wider, within the bound.
A program may use at most 128 MiB of HBM per device.

```python
import math
import jax
import jax.numpy as jnp
from jax import lax

C = 16
H = 128
W = 128
HID = 64
ITERS = 1
S = 32


def draw_coil_maps(key, part):
    shape = (2, S, C, H, W)
    samples = jax.random.normal(key, shape, jnp.float32)
    energy = jnp.sum(samples * samples, axis=(0, 2), keepdims=True)
    return (samples / jnp.sqrt(energy + 1e-06)).astype(jnp.bfloat16)


def touch_ends(array, rng, low, high):
    longest = array.shape.index(max(array.shape))
    spots = []
    for shift in (0, 1):
        where = [jax.random.randint(jax.random.fold_in(rng, axis), (), 0, length) for axis, length in enumerate(array.shape)]
        where[longest] = (where[longest] + shift) % array.shape[longest]
        spots.append(tuple(where))
    return array.at[spots[0]].set(low).at[spots[1]].set(high)


def shard_levels(key, extent, pieces, smallest, largest):
    level, own = 1.0, jax.random.fold_in(key, 6)
    for position, parts in pieces:
        draws = jnp.exp(jax.random.uniform(jax.random.fold_in(own, position), (parts,), jnp.float32, smallest / len(pieces), largest / len(pieces)))
        level = level * jnp.repeat(draws, extent[position] // parts).reshape([-1 if axis == position else 1 for axis in range(len(extent))])
    return level


def normal_values(rng, extent, spread, bound, split=(), kind=jnp.bfloat16):
    drawn = spread * jax.random.normal(rng, extent, jnp.float32)
    if split:
        drawn = drawn * shard_levels(rng, extent, split, -0.22, 0.18)
    return jnp.clip(drawn, -bound, bound).astype(kind)


def setup_inputs(seed: int = 0, part: int = 0) -> dict:
    splits = jax.random.split(jax.random.key(seed), 9)
    part_keys = jax.random.split(jax.random.fold_in(splits[8], part), 9)
    return {
        "kspace": normal_values(part_keys[0], (2, S, C, H * W), 1.0, 6.0, ((3, 16),)),
        "coil_maps": draw_coil_maps(jax.random.fold_in(jax.random.fold_in(splits[8], part), 71), part),
        "sample_mask": touch_ends((jax.random.randint(part_keys[2], (S, C, H), 0, 6) < 5).astype(jnp.int32), jax.random.fold_in(part_keys[2], 1), 0, 1),
        "tap_order": jax.random.permutation(splits[3], 27).astype(jnp.int32),
        "first_kernel": normal_values(splits[4], (27, 2, HID), 54 ** -0.5, 0.875),
        "first_bias": normal_values(splits[5], (HID,), 0.5, 2.0, (), jnp.float32),
        "second_kernel": normal_values(splits[6], (27, HID, 2), (27 * HID) ** -0.5, 0.15625),
        "second_bias": normal_values(splits[7], (2,), 0.5, 2.0, (), jnp.float32),
    }


def make_table(length, direction):
    positions = jnp.arange(length, dtype=jnp.int32)
    product = positions[:, None] * positions[None, :] % length
    angles = 2.0 * math.pi / length * product.astype(jnp.float32)
    norm_scale = 1.0 / math.sqrt(length)
    real_part = (jnp.cos(angles) * norm_scale).astype(jnp.bfloat16)
    imaginary = (direction * jnp.sin(angles) * norm_scale).astype(jnp.bfloat16)
    return (real_part, imaginary)

def transform(pattern, matrix, values):
    highest = lax.Precision.HIGHEST
    matrix_real = matrix[0].astype(jnp.float32)
    matrix_imag = matrix[1].astype(jnp.float32)
    value_real = values[0].astype(jnp.float32)
    value_imag = values[1].astype(jnp.float32)
    real_out = jnp.einsum(pattern, value_real, matrix_real, precision=highest) - jnp.einsum(pattern, value_imag, matrix_imag, precision=highest)
    imag_out = jnp.einsum(pattern, value_real, matrix_imag, precision=highest) + jnp.einsum(pattern, value_imag, matrix_real, precision=highest)
    return jnp.stack([real_out, imag_out])

def coil_forward(image, coil_map, tables):
    map_real = coil_map[0].astype(jnp.float32)
    map_imag = coil_map[1].astype(jnp.float32)
    coil_image = jnp.stack([map_real * image[0] - map_imag * image[1], map_real * image[1] + map_imag * image[0]]).astype(jnp.bfloat16)
    row_done = transform('zyj,kj->zyk', tables[0], coil_image).astype(jnp.bfloat16)
    plane = transform('zjx,kj->zkx', tables[1], row_done).astype(jnp.bfloat16)
    return transform('jyx,kj->kyx', tables[2], plane)

def coil_adjoint(residual, coil_map, tables):
    depth_back = transform('jyx,kj->kyx', tables[5], residual).astype(jnp.bfloat16)
    upward = transform('zjx,kj->zkx', tables[4], depth_back).astype(jnp.bfloat16)
    image_back = transform('zyj,kj->zyk', tables[3], upward)
    map_real = coil_map[0].astype(jnp.float32)
    map_imag = coil_map[1].astype(jnp.float32)
    return jnp.stack([map_real * image_back[0] + map_imag * image_back[1], map_real * image_back[1] - map_imag * image_back[0]])

def tap_kernel(tap_order, stored):
    chosen = (tap_order[None, :] == jnp.arange(27, dtype=jnp.int32)[:, None]).astype(jnp.float32)
    picked = jnp.einsum('tq,qio->tio', chosen, stored.astype(jnp.float32), precision=lax.Precision.HIGHEST)
    return picked.astype(jnp.bfloat16)

def volume_conv(values, kernel):
    weights = jnp.transpose(kernel.astype(jnp.float32).reshape(3, 3, 3, kernel.shape[1], kernel.shape[2]), (4, 3, 0, 1, 2))
    return lax.conv_general_dilated(values[None], weights, (1, 1, 1), ((1, 1), (1, 1), (1, 1)), dimension_numbers=('NCDHW', 'OIDHW', 'NCDHW'), precision=lax.Precision.HIGHEST)[0]

def denoise(field, kernel_one, first_bias, kernel_two, second_bias):
    field_low = lax.optimization_barrier(field.astype(jnp.bfloat16)).astype(jnp.float32)
    groups = HID // 8
    one_groups = jnp.transpose(kernel_one.reshape(27, 2, groups, 8), (2, 0, 1, 3))
    two_groups = jnp.transpose(kernel_two.reshape(27, groups, 8, 2), (1, 0, 2, 3))
    bias_groups = first_bias.reshape(groups, 8)

    def group_step(running, inputs):
        one_part, bias_part, two_part = inputs
        hidden = jax.nn.relu(volume_conv(field_low, one_part) + bias_part[:, None, None, None]).astype(jnp.bfloat16)
        hidden = lax.optimization_barrier(hidden)
        return (running + volume_conv(hidden.astype(jnp.float32), two_part), None)
    summed = lax.scan(group_step, jnp.zeros_like(field), (one_groups, bias_groups, two_groups))[0]
    return summed + second_bias[:, None, None, None]

def reference(kspace, coil_maps, sample_mask, tap_order, first_kernel, first_bias, second_kernel, second_bias):
    tables = (make_table(W, -1.0), make_table(H, -1.0), make_table(S, -1.0), make_table(W, 1.0), make_table(H, 1.0), make_table(S, 1.0))
    measured = jnp.moveaxis(kspace.reshape(2, S, C, H, W), 2, 0)
    maps_by_coil = jnp.moveaxis(coil_maps, 2, 0)
    sampled_lines = jnp.moveaxis(sample_mask, 1, 0).astype(jnp.float32)[:, None, :, :, None]
    empty_sum = jnp.zeros((2, S, H, W), jnp.float32)

    def data_step(running, inputs):
        measured_coil, map_coil, line_coil = inputs
        residual = (line_coil * measured_coil.astype(jnp.float32)).astype(jnp.bfloat16)
        return (running + coil_adjoint(residual, map_coil, tables), None)
    estimate = lax.scan(data_step, empty_sum, (measured, maps_by_coil, sampled_lines))[0]

    def normal_op(image):

        def coil_step(running, inputs):
            measured_coil, map_coil, line_coil = inputs
            spectrum = coil_forward(image, map_coil, tables)
            residual = (line_coil * (spectrum - measured_coil.astype(jnp.float32))).astype(jnp.bfloat16)
            return (running + coil_adjoint(residual, map_coil, tables), None)
        return lax.scan(coil_step, empty_sum, (measured, maps_by_coil, sampled_lines))[0]
    kernel_one = tap_kernel(tap_order, first_kernel)
    kernel_two = tap_kernel(tap_order, second_kernel)
    dual_var = jnp.zeros_like(estimate)
    for iteration in range(ITERS):
        before = estimate - dual_var
        update = before - normal_op(before)
        denoiser_in = update + dual_var
        estimate = denoiser_in - denoise(denoiser_in, kernel_one, first_bias, kernel_two, second_bias)
        dual_var = dual_var + update - estimate
    return (estimate, dual_var)
```

```python
import functools
import math

import jax
import jax.numpy as jnp
from jax import lax
from jax.experimental import pallas as pl
from jax.experimental.pallas import tpu as pltpu
from jax.sharding import PartitionSpec as P

C = 16
H = 128
W = 128


def padded_2(cells, sides, width):
    for axis, dim in sides:
        count = lax.axis_size(axis)
        ends = count - 1
        head = lax.slice_in_dim(cells, 0, width, axis=dim)
        tail = lax.slice_in_dim(cells, cells.shape[dim] - width, cells.shape[dim], axis=dim)
        cells = jnp.concatenate(
            [
                lax.ppermute(tail, axis, [(i, (i + 1) % count) for i in range(ends)]),
                cells,
                lax.ppermute(head, axis, [((i + 1) % count, i) for i in range(ends)]),
            ],
            axis=dim,
        )
    return cells


def make_table(length, direction):
    positions = jnp.arange(length, dtype=jnp.int32)
    product = positions[:, None] * positions[None, :] % length
    angles = 2.0 * math.pi / length * product.astype(jnp.float32)
    norm_scale = 1.0 / math.sqrt(length)
    real_part = (jnp.cos(angles) * norm_scale).astype(jnp.bfloat16)
    imaginary = (direction * jnp.sin(angles) * norm_scale).astype(jnp.bfloat16)
    real_t = jnp.transpose(real_part)
    imag_t = jnp.transpose(imaginary)
    upper = jnp.stack([real_t, imag_t], axis=1)
    lower = jnp.stack([-imag_t, real_t], axis=1)
    return jnp.stack([upper, lower])


def tap_kernel(tap_order, stored):
    chosen = (tap_order[None, :] == jnp.arange(27, dtype=jnp.int32)[:, None]).astype(jnp.bfloat16)
    return jnp.einsum("tq,qio->tio", chosen, stored, preferred_element_type=jnp.float32).astype(
        jnp.bfloat16
    )


def conv_kernel(
    depth, height, width, rows, columns_ref, one_ref, bias_ref, two_ref, out_bias_ref, noise_ref, terms
):
    block = rows * width
    group = noise_ref.shape[0]
    band = columns_ref.shape[0]
    lane = lax.broadcasted_iota(jnp.int32, (band, block), 1) % width
    out_lane = lax.broadcasted_iota(jnp.int32, (group, block), 1) % width
    terms[:, :width] = jnp.zeros((terms.shape[0], width), jnp.float32)
    terms[:, (height + 1) * width :] = jnp.zeros((terms.shape[0], width), jnp.float32)

    def hidden_step(step, carry):
        start = pl.multiple_of(step * block, block)
        parts = []
        for row_shift in range(3):
            here = columns_ref[:, pl.ds(pl.multiple_of(start + row_shift * width, width), block)]
            here = here.astype(jnp.float32)
            left = jnp.where(lane == 0, 0.0, pltpu.roll(here, 1, 1))
            right = jnp.where(lane == width - 1, 0.0, pltpu.roll(here, block - 1, 1))
            parts += [left, here, right]
        columns = jnp.concatenate([part.astype(jnp.bfloat16) for part in parts], axis=0)
        summed = jnp.dot(one_ref[...], columns, preferred_element_type=jnp.float32)
        hidden = jnp.maximum(summed + bias_ref[:, :1], 0.0) * bias_ref[:, 1:2]
        terms[:, pl.ds(pl.multiple_of(start + width, width), block)] = jnp.dot(
            two_ref[...], hidden.astype(jnp.bfloat16), preferred_element_type=jnp.float32
        )
        return carry

    lax.fori_loop(0, height // rows, hidden_step, 0)

    def sum_step(step, carry):
        start = pl.multiple_of(step * block, block)
        sums = []
        for column_shift in range(3):
            total = None
            for row_shift in range(3):
                first = (3 * row_shift + column_shift) * group
                piece = terms[
                    first : first + group,
                    pl.ds(pl.multiple_of(start + row_shift * width, width), block),
                ]
                total = piece if total is None else total + piece
            sums.append(total)
        left = jnp.where(out_lane == 0, 0.0, pltpu.roll(sums[0], 1, 1))
        right = jnp.where(out_lane == width - 1, 0.0, pltpu.roll(sums[2], block - 1, 1))
        noise_ref[:, pl.ds(start, block)] = left + sums[1] + right + out_bias_ref[:, :1]
        return carry

    lax.fori_loop(0, height // rows, sum_step, 0)


def denoise(widened, kernel_one, first_bias, kernel_two, second_bias, inside):
    channels, deep, height, width = widened.shape
    mid = deep - 2
    depth = deep - 4
    hid = first_bias.shape[0]
    band = -(-channels * deep // 16) * 16
    group = -(-channels * depth // 8) * 8
    columns = jnp.transpose(widened, (1, 0, 2, 3)).reshape(deep * channels, height * width)
    columns = jnp.pad(columns, ((0, band - deep * channels), (width, width)))
    taps = jnp.arange(3)
    place_one = (
        jnp.arange(deep)[None, :, None] == jnp.arange(mid)[:, None, None] + taps[None, None, :]
    ).astype(jnp.bfloat16)
    place_two = (
        jnp.arange(mid)[None, :, None] == jnp.arange(depth)[:, None, None] + taps[None, None, :]
    ).astype(jnp.bfloat16)
    one = jnp.einsum(
        "szd,dyxio->soyxzi",
        place_one,
        kernel_one.reshape(3, 3, 3, channels, hid),
        preferred_element_type=jnp.float32,
    ).astype(jnp.bfloat16)
    one = one.reshape(mid * hid, 9, deep * channels)
    one = jnp.pad(one, ((0, 0), (0, 0), (0, band - deep * channels))).reshape(mid * hid, 9 * band)
    two = jnp.einsum(
        "zsd,dyxho->yxzosh",
        place_two,
        kernel_two.reshape(3, 3, 3, hid, channels),
        preferred_element_type=jnp.float32,
    ).astype(jnp.bfloat16)
    two = two.reshape(9, depth * channels, mid * hid)
    two = jnp.pad(two, ((0, 0), (0, group - depth * channels), (0, 0))).reshape(9 * group, mid * hid)
    bias = jnp.stack([jnp.tile(first_bias, mid), jnp.repeat(inside.astype(jnp.float32), hid)], axis=1)
    out_bias = jnp.pad(jnp.tile(second_bias, depth), (0, group - depth * channels))[:, None]
    rows = math.gcd(8, height)
    noise = pl.pallas_call(
        functools.partial(conv_kernel, depth, height, width, rows),
        out_shape=jax.ShapeDtypeStruct((group, height * width), jnp.float32),
        in_specs=[pl.BlockSpec(memory_space=pltpu.VMEM)] * 5,
        out_specs=pl.BlockSpec(memory_space=pltpu.VMEM),
        scratch_shapes=[pltpu.VMEM((9 * group, (height + 2) * width), jnp.float32)],
        compiler_params=pltpu.CompilerParams(vmem_limit_bytes=32 * 1024 * 1024),
        name="denoise",
    )(columns, one, bias, two, out_bias)
    noise = noise[: depth * channels].reshape(depth, channels, height, width)
    return jnp.transpose(noise, (1, 0, 2, 3))


def on_device(
    kspace, coil_maps, sample_mask, tap_order, first_kernel, first_bias, second_kernel, second_bias
):
    position = lax.axis_index("slc")
    slab_depth = coil_maps.shape[1]
    slices = kspace.shape[1]
    points = kspace.shape[3]
    table_cols = make_table(W, -1.0)
    table_rows = make_table(H, -1.0)
    table_depth = make_table(slices, -1.0)
    inverse_cols = make_table(W, 1.0)
    inverse_rows = make_table(H, 1.0)
    inverse_depth = make_table(slices, 1.0)
    point_rows = (position * points + jnp.arange(points, dtype=jnp.int32)) // W
    row_picker = (point_rows[None, :] == jnp.arange(H, dtype=jnp.int32)[:, None]).astype(
        jnp.bfloat16
    )
    sampled = jnp.einsum(
        "zch,hp->zcp",
        sample_mask.astype(jnp.bfloat16),
        row_picker,
        preferred_element_type=jnp.float32,
    )
    count = slices // slab_depth
    own_rows = points // W
    measured = kspace.reshape(2, slices, C, own_rows, W).astype(jnp.float32)
    sampled = sampled.reshape(slices, C, own_rows, W)
    map_real = coil_maps[0]
    map_imag = coil_maps[1]

    def adjoint(residual):
        depth_back = jnp.einsum(
            "pjcrx,pjqk->kqcrx", residual, inverse_depth, preferred_element_type=jnp.float32
        ).astype(jnp.bfloat16)
        slabs = lax.all_to_all(depth_back, "slc", split_axis=0, concat_axis=0, tiled=True)
        slabs = slabs.reshape(count, slab_depth, 2, C, own_rows, W)
        slabs = jnp.transpose(slabs, (2, 1, 3, 0, 4, 5)).reshape(2, slab_depth, C, H, W)
        upward = jnp.einsum(
            "pscjx,pjqk->qsckx", slabs, inverse_rows, preferred_element_type=jnp.float32
        ).astype(jnp.bfloat16)
        image_back = jnp.einsum(
            "pscyj,pjqk->qscyk", upward, inverse_cols, preferred_element_type=jnp.float32
        )
        real_sum = jnp.sum(map_real * image_back[0] + map_imag * image_back[1], axis=1)
        imag_sum = jnp.sum(map_real * image_back[1] - map_imag * image_back[0], axis=1)
        return jnp.stack([real_sum, imag_sum])

    kernel_one = tap_kernel(tap_order, first_kernel)
    kernel_two = tap_kernel(tap_order, second_kernel)
    estimate = adjoint((sampled[None] * measured).astype(jnp.bfloat16))
    before = estimate
    image_real = before[0][:, None]
    image_imag = before[1][:, None]
    coil_image = jnp.stack(
        [
            map_real * image_real - map_imag * image_imag,
            map_real * image_imag + map_imag * image_real,
        ]
    ).astype(jnp.bfloat16)
    row_done = jnp.einsum(
        "pscyj,pjqk->qscyk", coil_image, table_cols, preferred_element_type=jnp.float32
    ).astype(jnp.bfloat16)
    plane = jnp.einsum(
        "pscjx,pjqk->qsckx", row_done, table_rows, preferred_element_type=jnp.float32
    ).astype(jnp.bfloat16)
    plane = plane.reshape(2, slab_depth, C, count, own_rows, W)
    plane = jnp.transpose(plane, (3, 1, 0, 2, 4, 5))
    pencil = lax.all_to_all(plane, "slc", split_axis=0, concat_axis=0, tiled=True)
    pencil = pencil.reshape(slices, 2, C, own_rows, W)
    spectrum = jnp.einsum(
        "jpcrx,pjqk->qkcrx", pencil, table_depth, preferred_element_type=jnp.float32
    )
    residual = (sampled[None] * (spectrum - measured)).astype(jnp.bfloat16)
    update = before - adjoint(residual)
    field_low = update.astype(jnp.bfloat16)
    widened = padded_2(field_low, (("slc", 1),), 2)
    global_slice = position * slab_depth - 1 + jnp.arange(slab_depth + 2, dtype=jnp.int32)
    inside = (global_slice >= 0) & (global_slice < slices)
    estimate = update - denoise(widened, kernel_one, first_bias, kernel_two, second_bias, inside)
    dual_var = update - estimate
    return (estimate, dual_var)


def solution(mesh):
    placed = (
        P("grp", None, None, "slc"),
        P("grp", "slc", None, None, None),
        P("grp", None, None),
        P(),
        P(),
        P(),
        P(),
        P(),
    )
    return jax.shard_map(
        on_device,
        mesh=mesh,
        in_specs=placed,
        out_specs=(P("grp", "slc", None, None), P("grp", "slc", None, None)),
        check_vma=False,
    )
```

```python
import functools
import math

import jax
import jax.numpy as jnp
from jax import lax
from jax.experimental import pallas as pl
from jax.experimental.pallas import tpu as pltpu
from jax.sharding import PartitionSpec as P

C = 16
H = 128
W = 128


def padded_2(cells, sides, width):
    for axis, dim in sides:
        count = lax.axis_size(axis)
        ends = count - 1
        head = lax.slice_in_dim(cells, 0, width, axis=dim)
        tail = lax.slice_in_dim(cells, cells.shape[dim] - width, cells.shape[dim], axis=dim)
        cells = jnp.concatenate(
            [
                lax.ppermute(tail, axis, [(i, (i + 1) % count) for i in range(ends)]),
                cells,
                lax.ppermute(head, axis, [((i + 1) % count, i) for i in range(ends)]),
            ],
            axis=dim,
        )
    return cells


def make_table(length, direction):
    positions = jnp.arange(length, dtype=jnp.int32)
    product = positions[:, None] * positions[None, :] % length
    angles = 2.0 * math.pi / length * product.astype(jnp.float32)
    norm_scale = 1.0 / math.sqrt(length)
    real_part = (jnp.cos(angles) * norm_scale).astype(jnp.bfloat16)
    imaginary = (direction * jnp.sin(angles) * norm_scale).astype(jnp.bfloat16)
    real_t = jnp.transpose(real_part)
    imag_t = jnp.transpose(imaginary)
    upper = jnp.stack([real_t, imag_t], axis=1)
    lower = jnp.stack([-imag_t, real_t], axis=1)
    return jnp.stack([upper, lower])


def tap_kernel(tap_order, stored):
    chosen = (tap_order[None, :] == jnp.arange(27, dtype=jnp.int32)[:, None]).astype(jnp.bfloat16)
    return jnp.einsum("tq,qio->tio", chosen, stored, preferred_element_type=jnp.float32).astype(
        jnp.bfloat16
    )


def conv_kernel(
    depth, height, width, rows, columns_ref, one_ref, bias_ref, two_ref, out_bias_ref, noise_ref, terms
):
    block = rows * width
    group = noise_ref.shape[0]
    band = columns_ref.shape[0]
    lane = lax.broadcasted_iota(jnp.int32, (band, block), 1) % width
    out_lane = lax.broadcasted_iota(jnp.int32, (group, block), 1) % width
    terms[:, :width] = jnp.zeros((terms.shape[0], width), jnp.float32)
    terms[:, (height + 1) * width :] = jnp.zeros((terms.shape[0], width), jnp.float32)

    def hidden_step(step, carry):
        start = pl.multiple_of(step * block, block)
        parts = []
        for row_shift in range(3):
            here = columns_ref[:, pl.ds(pl.multiple_of(start + row_shift * width, width), block)]
            here = here.astype(jnp.float32)
            left = jnp.where(lane == 0, 0.0, pltpu.roll(here, 1, 1))
            right = jnp.where(lane == width - 1, 0.0, pltpu.roll(here, block - 1, 1))
            parts += [left, here, right]
        columns = jnp.concatenate([part.astype(jnp.bfloat16) for part in parts], axis=0)
        summed = jnp.dot(one_ref[...], columns, preferred_element_type=jnp.float32)
        hidden = jnp.maximum(summed + bias_ref[:, :1], 0.0) * bias_ref[:, 1:2]
        terms[:, pl.ds(pl.multiple_of(start + width, width), block)] = jnp.dot(
            two_ref[...], hidden.astype(jnp.bfloat16), preferred_element_type=jnp.float32
        )
        return carry

    lax.fori_loop(0, height // rows, hidden_step, 0)

    def sum_step(step, carry):
        start = pl.multiple_of(step * block, block)
        sums = []
        for column_shift in range(3):
            total = None
            for row_shift in range(3):
                first = (3 * row_shift + column_shift) * group
                piece = terms[
                    first : first + group,
                    pl.ds(pl.multiple_of(start + row_shift * width, width), block),
                ]
                total = piece if total is None else total + piece
            sums.append(total)
        left = jnp.where(out_lane == 0, 0.0, pltpu.roll(sums[0], 1, 1))
        right = jnp.where(out_lane == width - 1, 0.0, pltpu.roll(sums[2], block - 1, 1))
        noise_ref[:, pl.ds(start, block)] = left + sums[1] + right + out_bias_ref[:, :1]
        return carry

    lax.fori_loop(0, height // rows, sum_step, 0)


def denoise(widened, kernel_one, first_bias, kernel_two, second_bias, inside):
    channels, deep, height, width = widened.shape
    mid = deep - 2
    depth = deep - 4
    hid = first_bias.shape[0]
    band = -(-channels * deep // 16) * 16
    group = -(-channels * depth // 8) * 8
    columns = jnp.transpose(widened, (1, 0, 2, 3)).reshape(deep * channels, height * width)
    columns = jnp.pad(columns, ((0, band - deep * channels), (width, width)))
    taps = jnp.arange(3)
    place_one = (
        jnp.arange(deep)[None, :, None] == jnp.arange(mid)[:, None, None] + taps[None, None, :]
    ).astype(jnp.bfloat16)
    place_two = (
        jnp.arange(mid)[None, :, None] == jnp.arange(depth)[:, None, None] + taps[None, None, :]
    ).astype(jnp.bfloat16)
    one = jnp.einsum(
        "szd,dyxio->soyxzi",
        place_one,
        kernel_one.reshape(3, 3, 3, channels, hid),
        preferred_element_type=jnp.float32,
    ).astype(jnp.bfloat16)
    one = one.reshape(mid * hid, 9, deep * channels)
    one = jnp.pad(one, ((0, 0), (0, 0), (0, band - deep * channels))).reshape(mid * hid, 9 * band)
    two = jnp.einsum(
        "zsd,dyxho->yxzosh",
        place_two,
        kernel_two.reshape(3, 3, 3, hid, channels),
        preferred_element_type=jnp.float32,
    ).astype(jnp.bfloat16)
    two = two.reshape(9, depth * channels, mid * hid)
    two = jnp.pad(two, ((0, 0), (0, group - depth * channels), (0, 0))).reshape(9 * group, mid * hid)
    bias = jnp.stack([jnp.tile(first_bias, mid), jnp.repeat(inside.astype(jnp.float32), hid)], axis=1)
    out_bias = jnp.pad(jnp.tile(second_bias, depth), (0, group - depth * channels))[:, None]
    rows = math.gcd(8, height)
    noise = pl.pallas_call(
        functools.partial(conv_kernel, depth, height, width, rows),
        out_shape=jax.ShapeDtypeStruct((group, height * width), jnp.float32),
        in_specs=[pl.BlockSpec(memory_space=pltpu.VMEM)] * 5,
        out_specs=pl.BlockSpec(memory_space=pltpu.VMEM),
        scratch_shapes=[pltpu.VMEM((9 * group, (height + 2) * width), jnp.float32)],
        compiler_params=pltpu.CompilerParams(vmem_limit_bytes=32 * 1024 * 1024),
        name="denoise",
    )(columns, one, bias, two, out_bias)
    noise = noise[: depth * channels].reshape(depth, channels, height, width)
    return jnp.transpose(noise, (1, 0, 2, 3))


def on_device(
    kspace, coil_maps, sample_mask, tap_order, first_kernel, first_bias, second_kernel, second_bias
):
    position = lax.axis_index("slc")
    slab_depth = coil_maps.shape[1]
    slices = kspace.shape[1]
    points = kspace.shape[3]
    table_cols = make_table(W, -1.0)
    table_rows = make_table(H, -1.0)
    table_depth = make_table(slices, -1.0)
    inverse_cols = make_table(W, 1.0)
    inverse_rows = make_table(H, 1.0)
    inverse_depth = make_table(slices, 1.0)
    point_rows = (position * points + jnp.arange(points, dtype=jnp.int32)) // W
    row_picker = (point_rows[None, :] == jnp.arange(H, dtype=jnp.int32)[:, None]).astype(
        jnp.bfloat16
    )
    sampled = jnp.einsum(
        "zch,hp->zcp",
        sample_mask.astype(jnp.bfloat16),
        row_picker,
        preferred_element_type=jnp.float32,
    )
    count = slices // slab_depth
    own_rows = points // W
    measured = kspace.reshape(2, slices, C, own_rows, W).astype(jnp.float32)
    sampled = sampled.reshape(slices, C, own_rows, W)
    map_real = coil_maps[0]
    map_imag = coil_maps[1]

    def adjoint(residual):
        depth_back = jnp.einsum(
            "pjcrx,pjqk->kqcrx", residual, inverse_depth, preferred_element_type=jnp.float32
        ).astype(jnp.bfloat16)
        slabs = lax.all_to_all(depth_back, "slc", split_axis=0, concat_axis=0, tiled=True)
        slabs = slabs.reshape(count, slab_depth, 2, C, own_rows, W)
        slabs = jnp.transpose(slabs, (2, 1, 3, 0, 4, 5)).reshape(2, slab_depth, C, H, W)
        upward = jnp.einsum(
            "pscjx,pjqk->qsckx", slabs, inverse_rows, preferred_element_type=jnp.float32
        ).astype(jnp.bfloat16)
        image_back = jnp.einsum(
            "pscyj,pjqk->qscyk", upward, inverse_cols, preferred_element_type=jnp.float32
        )
        real_sum = jnp.sum(map_real * image_back[0] + map_imag * image_back[1], axis=1)
        imag_sum = jnp.sum(map_real * image_back[1] - map_imag * image_back[0], axis=1)
        return jnp.stack([real_sum, imag_sum])

    def point_normal(before):
        image_real = before[0][:, None]
        image_imag = before[1][:, None]
        coil_image = jnp.stack(
            [
                map_real * image_real - map_imag * image_imag,
                map_real * image_imag + map_imag * image_real,
            ]
        ).astype(jnp.bfloat16)
        row_done = jnp.einsum(
            "pscyj,pjqk->qscyk", coil_image, table_cols, preferred_element_type=jnp.float32
        ).astype(jnp.bfloat16)
        plane = jnp.einsum(
            "pscjx,pjqk->qsckx", row_done, table_rows, preferred_element_type=jnp.float32
        ).astype(jnp.bfloat16)
        plane = plane.reshape(2, slab_depth, C, count, own_rows, W)
        plane = jnp.transpose(plane, (3, 1, 0, 2, 4, 5))
        pencil = lax.all_to_all(plane, "slc", split_axis=0, concat_axis=0, tiled=True)
        pencil = pencil.reshape(slices, 2, C, own_rows, W)
        spectrum = jnp.einsum(
            "jpcrx,pjqk->qkcrx", pencil, table_depth, preferred_element_type=jnp.float32
        )
        residual = (sampled[None] * (spectrum - measured)).astype(jnp.bfloat16)
        return adjoint(residual)

    def coil_normal(before):
        own_coils = C // count
        maps = jnp.transpose(coil_maps, (2, 0, 1, 3, 4))
        maps = lax.all_to_all(maps, "slc", split_axis=0, concat_axis=0, tiled=True)
        maps = maps.reshape(count, own_coils, 2, slab_depth, H, W)
        maps = jnp.transpose(maps, (2, 0, 3, 1, 4, 5)).reshape(2, slices, own_coils, H, W)
        own_real, own_imag = maps[0], maps[1]
        mask = lax.dynamic_slice_in_dim(sample_mask, position * own_coils, own_coils, axis=1)
        image = lax.all_gather(before.astype(jnp.bfloat16), "slc", axis=1, tiled=True)
        image_real = image[0][:, None].astype(jnp.float32)
        image_imag = image[1][:, None].astype(jnp.float32)
        coil_image = jnp.stack(
            [
                own_real * image_real - own_imag * image_imag,
                own_real * image_imag + own_imag * image_real,
            ]
        ).astype(jnp.bfloat16)
        row_done = jnp.einsum(
            "pscyj,pjqk->qscyk", coil_image, table_cols, preferred_element_type=jnp.float32
        ).astype(jnp.bfloat16)
        plane = jnp.einsum(
            "pscjx,pjqk->qsckx", row_done, table_rows, preferred_element_type=jnp.float32
        ).astype(jnp.bfloat16)
        spectrum = jnp.einsum(
            "pjcyx,pjqk->qkcyx", plane, table_depth, preferred_element_type=jnp.float32
        )
        residual = (mask.astype(jnp.float32)[None, ..., None] * spectrum).astype(jnp.bfloat16)
        depth_back = jnp.einsum(
            "pjcyx,pjqk->qkcyx", residual, inverse_depth, preferred_element_type=jnp.float32
        ).astype(jnp.bfloat16)
        upward = jnp.einsum(
            "pscjx,pjqk->qsckx", depth_back, inverse_rows, preferred_element_type=jnp.float32
        ).astype(jnp.bfloat16)
        image_back = jnp.einsum(
            "pscyj,pjqk->qscyk", upward, inverse_cols, preferred_element_type=jnp.float32
        )
        real_sum = jnp.sum(own_real * image_back[0] + own_imag * image_back[1], axis=1)
        imag_sum = jnp.sum(own_real * image_back[1] - own_imag * image_back[0], axis=1)
        partial = jnp.stack([real_sum, imag_sum], axis=1).astype(jnp.bfloat16)
        total = lax.psum_scatter(partial, "slc", scatter_dimension=0, tiled=True)
        return jnp.transpose(total.astype(jnp.float32), (1, 0, 2, 3))

    kernel_one = tap_kernel(tap_order, first_kernel)
    kernel_two = tap_kernel(tap_order, second_kernel)
    estimate = adjoint((sampled[None] * measured).astype(jnp.bfloat16))
    before = estimate
    if C % count == 0:
        update = before + estimate - coil_normal(before)
    else:
        update = before - point_normal(before)
    field_low = update.astype(jnp.bfloat16)
    widened = padded_2(field_low, (("slc", 1),), 2)
    global_slice = position * slab_depth - 1 + jnp.arange(slab_depth + 2, dtype=jnp.int32)
    inside = (global_slice >= 0) & (global_slice < slices)
    estimate = update - denoise(widened, kernel_one, first_bias, kernel_two, second_bias, inside)
    dual_var = update - estimate
    return (estimate, dual_var)


def solution(mesh):
    placed = (
        P("grp", None, None, "slc"),
        P("grp", "slc", None, None, None),
        P("grp", None, None),
        P(),
        P(),
        P(),
        P(),
        P(),
    )
    return jax.shard_map(
        on_device,
        mesh=mesh,
        in_specs=placed,
        out_specs=(P("grp", "slc", None, None), P("grp", "slc", None, None)),
        check_vma=False,
    )
```

```python
import functools
import math

import jax
import jax.numpy as jnp
from jax import lax
from jax.experimental import pallas as pl
from jax.experimental.pallas import tpu as pltpu
from jax.sharding import PartitionSpec as P

C = 16
H = 128
W = 128


def padded_2(cells, sides, width):
    for axis, dim in sides:
        count = lax.axis_size(axis)
        ends = count - 1
        head = lax.slice_in_dim(cells, 0, width, axis=dim)
        tail = lax.slice_in_dim(cells, cells.shape[dim] - width, cells.shape[dim], axis=dim)
        cells = jnp.concatenate(
            [
                lax.ppermute(tail, axis, [(i, (i + 1) % count) for i in range(ends)]),
                cells,
                lax.ppermute(head, axis, [((i + 1) % count, i) for i in range(ends)]),
            ],
            axis=dim,
        )
    return cells


def make_table(length, direction):
    positions = jnp.arange(length, dtype=jnp.int32)
    product = positions[:, None] * positions[None, :] % length
    angles = 2.0 * math.pi / length * product.astype(jnp.float32)
    norm_scale = 1.0 / math.sqrt(length)
    real_part = (jnp.cos(angles) * norm_scale).astype(jnp.bfloat16)
    imaginary = (direction * jnp.sin(angles) * norm_scale).astype(jnp.bfloat16)
    real_t = jnp.transpose(real_part)
    imag_t = jnp.transpose(imaginary)
    upper = jnp.stack([real_t, imag_t], axis=1)
    lower = jnp.stack([-imag_t, real_t], axis=1)
    return jnp.stack([upper, lower])


def tap_kernel(tap_order, stored):
    chosen = (tap_order[None, :] == jnp.arange(27, dtype=jnp.int32)[:, None]).astype(jnp.bfloat16)
    return jnp.einsum("tq,qio->tio", chosen, stored, preferred_element_type=jnp.float32).astype(
        jnp.bfloat16
    )


def conv_kernel(
    depth, height, width, rows, columns_ref, one_ref, bias_ref, two_ref, out_bias_ref, noise_ref, terms
):
    block = rows * width
    group = noise_ref.shape[0]
    band = columns_ref.shape[0]
    lane = lax.broadcasted_iota(jnp.int32, (band, block), 1) % width
    out_lane = lax.broadcasted_iota(jnp.int32, (group, block), 1) % width
    terms[:, :width] = jnp.zeros((terms.shape[0], width), jnp.float32)
    terms[:, (height + 1) * width :] = jnp.zeros((terms.shape[0], width), jnp.float32)

    def hidden_step(step, carry):
        start = pl.multiple_of(step * block, block)
        parts = []
        for row_shift in range(3):
            here = columns_ref[:, pl.ds(pl.multiple_of(start + row_shift * width, width), block)]
            here = here.astype(jnp.float32)
            left = jnp.where(lane == 0, 0.0, pltpu.roll(here, 1, 1))
            right = jnp.where(lane == width - 1, 0.0, pltpu.roll(here, block - 1, 1))
            parts += [left, here, right]
        columns = jnp.concatenate([part.astype(jnp.bfloat16) for part in parts], axis=0)
        summed = jnp.dot(one_ref[...], columns, preferred_element_type=jnp.float32)
        hidden = jnp.maximum(summed + bias_ref[:, :1], 0.0) * bias_ref[:, 1:2]
        terms[:, pl.ds(pl.multiple_of(start + width, width), block)] = jnp.dot(
            two_ref[...], hidden.astype(jnp.bfloat16), preferred_element_type=jnp.float32
        )
        return carry

    lax.fori_loop(0, height // rows, hidden_step, 0)

    def sum_step(step, carry):
        start = pl.multiple_of(step * block, block)
        sums = []
        for column_shift in range(3):
            total = None
            for row_shift in range(3):
                first = (3 * row_shift + column_shift) * group
                piece = terms[
                    first : first + group,
                    pl.ds(pl.multiple_of(start + row_shift * width, width), block),
                ]
                total = piece if total is None else total + piece
            sums.append(total)
        left = jnp.where(out_lane == 0, 0.0, pltpu.roll(sums[0], 1, 1))
        right = jnp.where(out_lane == width - 1, 0.0, pltpu.roll(sums[2], block - 1, 1))
        noise_ref[:, pl.ds(start, block)] = left + sums[1] + right + out_bias_ref[:, :1]
        return carry

    lax.fori_loop(0, height // rows, sum_step, 0)


def denoise(widened, kernel_one, first_bias, kernel_two, second_bias, inside):
    channels, deep, height, width = widened.shape
    mid = deep - 2
    depth = deep - 4
    hid = first_bias.shape[0]
    band = -(-channels * deep // 16) * 16
    group = -(-channels * depth // 8) * 8
    columns = jnp.transpose(widened, (1, 0, 2, 3)).reshape(deep * channels, height * width)
    columns = jnp.pad(columns, ((0, band - deep * channels), (width, width)))
    taps = jnp.arange(3)
    place_one = (
        jnp.arange(deep)[None, :, None] == jnp.arange(mid)[:, None, None] + taps[None, None, :]
    ).astype(jnp.bfloat16)
    place_two = (
        jnp.arange(mid)[None, :, None] == jnp.arange(depth)[:, None, None] + taps[None, None, :]
    ).astype(jnp.bfloat16)
    one = jnp.einsum(
        "szd,dyxio->soyxzi",
        place_one,
        kernel_one.reshape(3, 3, 3, channels, hid),
        preferred_element_type=jnp.float32,
    ).astype(jnp.bfloat16)
    one = one.reshape(mid * hid, 9, deep * channels)
    one = jnp.pad(one, ((0, 0), (0, 0), (0, band - deep * channels))).reshape(mid * hid, 9 * band)
    two = jnp.einsum(
        "zsd,dyxho->yxzosh",
        place_two,
        kernel_two.reshape(3, 3, 3, hid, channels),
        preferred_element_type=jnp.float32,
    ).astype(jnp.bfloat16)
    two = two.reshape(9, depth * channels, mid * hid)
    two = jnp.pad(two, ((0, 0), (0, group - depth * channels), (0, 0))).reshape(9 * group, mid * hid)
    bias = jnp.stack([jnp.tile(first_bias, mid), jnp.repeat(inside.astype(jnp.float32), hid)], axis=1)
    out_bias = jnp.pad(jnp.tile(second_bias, depth), (0, group - depth * channels))[:, None]
    rows = math.gcd(8, height)
    noise = pl.pallas_call(
        functools.partial(conv_kernel, depth, height, width, rows),
        out_shape=jax.ShapeDtypeStruct((group, height * width), jnp.float32),
        in_specs=[pl.BlockSpec(memory_space=pltpu.VMEM)] * 5,
        out_specs=pl.BlockSpec(memory_space=pltpu.VMEM),
        scratch_shapes=[pltpu.VMEM((9 * group, (height + 2) * width), jnp.float32)],
        compiler_params=pltpu.CompilerParams(vmem_limit_bytes=32 * 1024 * 1024),
        name="denoise",
    )(columns, one, bias, two, out_bias)
    noise = noise[: depth * channels].reshape(depth, channels, height, width)
    return jnp.transpose(noise, (1, 0, 2, 3))


def scatter_kernel(bits, partial_ref, total_ref, *scratch):
    arrived, (send_sem, recv_sem) = scratch[:-2], scratch[-2:]
    me = lax.axis_index("slc")
    mine = [me // 2**bit % 2 for bit in range(bits)]
    partner = [me + (1 - 2 * mine[bit]) * 2**bit for bit in range(bits)]
    half = partial_ref.shape[-2] // 2
    orders = [list(range(bits)), [0, *range(2, bits), 1][:bits]]

    barrier = pltpu.get_barrier_semaphore()
    for bit in range(bits):
        pl.semaphore_signal(
            barrier, inc=1, device_id={"slc": partner[bit]}, device_id_type=pl.DeviceIdType.MESH
        )
    pl.semaphore_wait(barrier, bits)

    held = [partial_ref.at[..., pl.ds(chain * half, half), :] for chain in range(2)]
    left = [list(range(bits - 1, -1, -1)) for _ in range(2)]
    copies = [[], []]

    def part(chain, bit, choice):
        place = left[chain].index(bit)
        return held[chain].at[(slice(None),) * place + (choice,)]

    def send(chain, step):
        bit = orders[chain][step]
        copy = pltpu.make_async_remote_copy(
            src_ref=part(chain, bit, 1 - mine[bit]),
            dst_ref=arrived[chain * bits + step],
            send_sem=send_sem.at[chain, step],
            recv_sem=recv_sem.at[chain, step],
            device_id={"slc": partner[bit]},
            device_id_type=pl.DeviceIdType.MESH,
        )
        copy.start()
        copies[chain].append(copy)

    for chain in range(2):
        send(chain, 0)
    for step in range(bits):
        for chain in range(2):
            bit = orders[chain][step]
            landed = arrived[chain * bits + step]
            copies[chain][step].wait_recv()
            kept = part(chain, bit, mine[bit])[...].astype(jnp.float32)
            summed = kept + landed[...].astype(jnp.float32)
            if step == bits - 1:
                total_ref[chain * half : (chain + 1) * half, :] = summed
            else:
                landed[...] = summed.astype(landed.dtype)
                held[chain] = landed
                left[chain].remove(bit)
                send(chain, step + 1)
    for chain in range(2):
        for copy in copies[chain]:
            copy.wait_send()


def sum_scatter(partial):
    count, rows, width = partial.shape
    bits = count.bit_length() - 1
    landing = [
        pltpu.VMEM((2,) * (bits - 1 - step) + (rows // 2, width), partial.dtype)
        for _ in range(2)
        for step in range(bits)
    ]
    return pl.pallas_call(
        functools.partial(scatter_kernel, bits),
        out_shape=jax.ShapeDtypeStruct((rows, width), jnp.float32),
        in_specs=[pl.BlockSpec(memory_space=pltpu.VMEM)],
        out_specs=pl.BlockSpec(memory_space=pltpu.VMEM),
        scratch_shapes=landing
        + [pltpu.SemaphoreType.DMA((2, bits)), pltpu.SemaphoreType.DMA((2, bits))],
        compiler_params=pltpu.CompilerParams(
            collective_id=0, has_side_effects=True, vmem_limit_bytes=32 * 1024 * 1024
        ),
        name="sum_scatter",
    )(partial.reshape((2,) * bits + (rows, width)))


def on_device(
    kspace, coil_maps, sample_mask, tap_order, first_kernel, first_bias, second_kernel, second_bias
):
    position = lax.axis_index("slc")
    slab_depth = coil_maps.shape[1]
    slices = kspace.shape[1]
    points = kspace.shape[3]
    table_cols = make_table(W, -1.0)
    table_rows = make_table(H, -1.0)
    table_depth = make_table(slices, -1.0)
    inverse_cols = make_table(W, 1.0)
    inverse_rows = make_table(H, 1.0)
    inverse_depth = make_table(slices, 1.0)
    point_rows = (position * points + jnp.arange(points, dtype=jnp.int32)) // W
    row_picker = (point_rows[None, :] == jnp.arange(H, dtype=jnp.int32)[:, None]).astype(
        jnp.bfloat16
    )
    sampled = jnp.einsum(
        "zch,hp->zcp",
        sample_mask.astype(jnp.bfloat16),
        row_picker,
        preferred_element_type=jnp.float32,
    )
    count = slices // slab_depth
    own_rows = points // W
    measured = kspace.reshape(2, slices, C, own_rows, W).astype(jnp.float32)
    sampled = sampled.reshape(slices, C, own_rows, W)
    map_real = coil_maps[0]
    map_imag = coil_maps[1]

    def adjoint(residual, first=None):
        depth_back = jnp.einsum(
            "pjcrx,pjqk->kqcrx", residual, inverse_depth, preferred_element_type=jnp.float32
        ).astype(jnp.bfloat16)
        if first is not None:
            depth_back, _ = lax.optimization_barrier((depth_back, first))
        slabs = lax.all_to_all(depth_back, "slc", split_axis=0, concat_axis=0, tiled=True)
        slabs = slabs.reshape(count, slab_depth, 2, C, own_rows, W)
        slabs = jnp.transpose(slabs, (2, 1, 3, 0, 4, 5)).reshape(2, slab_depth, C, H, W)
        upward = jnp.einsum(
            "pscjx,pjqk->qsckx", slabs, inverse_rows, preferred_element_type=jnp.float32
        ).astype(jnp.bfloat16)
        image_back = jnp.einsum(
            "pscyj,pjqk->qscyk", upward, inverse_cols, preferred_element_type=jnp.float32
        )
        real_sum = jnp.sum(map_real * image_back[0] + map_imag * image_back[1], axis=1)
        imag_sum = jnp.sum(map_real * image_back[1] - map_imag * image_back[0], axis=1)
        return jnp.stack([real_sum, imag_sum])

    def point_normal(before):
        image_real = before[0][:, None]
        image_imag = before[1][:, None]
        coil_image = jnp.stack(
            [
                map_real * image_real - map_imag * image_imag,
                map_real * image_imag + map_imag * image_real,
            ]
        ).astype(jnp.bfloat16)
        row_done = jnp.einsum(
            "pscyj,pjqk->qscyk", coil_image, table_cols, preferred_element_type=jnp.float32
        ).astype(jnp.bfloat16)
        plane = jnp.einsum(
            "pscjx,pjqk->qsckx", row_done, table_rows, preferred_element_type=jnp.float32
        ).astype(jnp.bfloat16)
        plane = plane.reshape(2, slab_depth, C, count, own_rows, W)
        plane = jnp.transpose(plane, (3, 1, 0, 2, 4, 5))
        pencil = lax.all_to_all(plane, "slc", split_axis=0, concat_axis=0, tiled=True)
        pencil = pencil.reshape(slices, 2, C, own_rows, W)
        spectrum = jnp.einsum(
            "jpcrx,pjqk->qkcrx", pencil, table_depth, preferred_element_type=jnp.float32
        )
        residual = (sampled[None] * (spectrum - measured)).astype(jnp.bfloat16)
        return adjoint(residual)

    def coil_normal(before):
        own_coils = C // count
        maps = maps_by_coil
        maps = maps.reshape(count, own_coils, 2, slab_depth, H, W)
        maps = jnp.transpose(maps, (2, 0, 3, 1, 4, 5)).reshape(2, slices, own_coils, H, W)
        own_real, own_imag = maps[0], maps[1]
        mask = lax.dynamic_slice_in_dim(sample_mask, position * own_coils, own_coils, axis=1)
        image = lax.all_gather(before.astype(jnp.bfloat16), "slc", axis=1, tiled=True)
        image_real = image[0][:, None].astype(jnp.float32)
        image_imag = image[1][:, None].astype(jnp.float32)
        coil_image = jnp.stack(
            [
                own_real * image_real - own_imag * image_imag,
                own_real * image_imag + own_imag * image_real,
            ]
        ).astype(jnp.bfloat16)
        row_done = jnp.einsum(
            "pscyj,pjqk->qscyk", coil_image, table_cols, preferred_element_type=jnp.float32
        ).astype(jnp.bfloat16)
        plane = jnp.einsum(
            "pscjx,pjqk->qsckx", row_done, table_rows, preferred_element_type=jnp.float32
        ).astype(jnp.bfloat16)
        spectrum = jnp.einsum(
            "pjcyx,pjqk->qkcyx", plane, table_depth, preferred_element_type=jnp.float32
        )
        residual = (mask.astype(jnp.float32)[None, ..., None] * spectrum).astype(jnp.bfloat16)
        depth_back = jnp.einsum(
            "pjcyx,pjqk->qkcyx", residual, inverse_depth, preferred_element_type=jnp.float32
        ).astype(jnp.bfloat16)
        upward = jnp.einsum(
            "pscjx,pjqk->qsckx", depth_back, inverse_rows, preferred_element_type=jnp.float32
        ).astype(jnp.bfloat16)
        image_back = jnp.einsum(
            "pscyj,pjqk->qscyk", upward, inverse_cols, preferred_element_type=jnp.float32
        )
        real_sum = jnp.sum(own_real * image_back[0] + own_imag * image_back[1], axis=1)
        imag_sum = jnp.sum(own_real * image_back[1] - own_imag * image_back[0], axis=1)
        partial = jnp.stack([real_sum, imag_sum], axis=1).astype(jnp.bfloat16)
        total = sum_scatter(partial.reshape(count, slab_depth * 2 * H, W))
        return jnp.transpose(total.reshape(slab_depth, 2, H, W), (1, 0, 2, 3))

    kernel_one = tap_kernel(tap_order, first_kernel)
    kernel_two = tap_kernel(tap_order, second_kernel)
    by_coil = C % count == 0 and count > 1 and count & (count - 1) == 0
    data = (sampled[None] * measured).astype(jnp.bfloat16)
    if by_coil:
        maps_by_coil = jnp.transpose(coil_maps, (2, 0, 1, 3, 4))
        maps_by_coil = lax.all_to_all(
            maps_by_coil, "slc", split_axis=0, concat_axis=0, tiled=True
        )
    estimate = adjoint(data, maps_by_coil if by_coil else None)
    before = estimate
    if by_coil:
        update = before + estimate - coil_normal(before)
    else:
        update = before - point_normal(before)
    field_low = update.astype(jnp.bfloat16)
    widened = padded_2(field_low, (("slc", 1),), 2)
    global_slice = position * slab_depth - 1 + jnp.arange(slab_depth + 2, dtype=jnp.int32)
    inside = (global_slice >= 0) & (global_slice < slices)
    estimate = update - denoise(widened, kernel_one, first_bias, kernel_two, second_bias, inside)
    dual_var = update - estimate
    return (estimate, dual_var)


def solution(mesh):
    placed = (
        P("grp", None, None, "slc"),
        P("grp", "slc", None, None, None),
        P("grp", None, None),
        P(),
        P(),
        P(),
        P(),
        P(),
    )
    return jax.shard_map(
        on_device,
        mesh=mesh,
        in_specs=placed,
        out_specs=(P("grp", "slc", None, None), P("grp", "slc", None, None)),
        check_vma=False,
    )
```

```python
import functools
import math

import jax
import jax.numpy as jnp
from jax import lax
from jax.experimental import pallas as pl
from jax.experimental.pallas import tpu as pltpu
from jax.sharding import PartitionSpec as P

C = 16
H = 128
W = 128


def padded_2(cells, sides, width):
    for axis, dim in sides:
        count = lax.axis_size(axis)
        ends = count - 1
        head = lax.slice_in_dim(cells, 0, width, axis=dim)
        tail = lax.slice_in_dim(cells, cells.shape[dim] - width, cells.shape[dim], axis=dim)
        cells = jnp.concatenate(
            [
                lax.ppermute(tail, axis, [(i, (i + 1) % count) for i in range(ends)]),
                cells,
                lax.ppermute(head, axis, [((i + 1) % count, i) for i in range(ends)]),
            ],
            axis=dim,
        )
    return cells


def make_table(length, direction):
    positions = jnp.arange(length, dtype=jnp.int32)
    product = positions[:, None] * positions[None, :] % length
    angles = 2.0 * math.pi / length * product.astype(jnp.float32)
    norm_scale = 1.0 / math.sqrt(length)
    real_part = (jnp.cos(angles) * norm_scale).astype(jnp.bfloat16)
    imaginary = (direction * jnp.sin(angles) * norm_scale).astype(jnp.bfloat16)
    real_t = jnp.transpose(real_part)
    imag_t = jnp.transpose(imaginary)
    upper = jnp.stack([real_t, imag_t], axis=1)
    lower = jnp.stack([-imag_t, real_t], axis=1)
    return jnp.stack([upper, lower])


def tap_kernel(tap_order, stored):
    chosen = (tap_order[None, :] == jnp.arange(27, dtype=jnp.int32)[:, None]).astype(jnp.bfloat16)
    return jnp.einsum("tq,qio->tio", chosen, stored, preferred_element_type=jnp.float32).astype(
        jnp.bfloat16
    )


def conv_kernel(
    depth, height, width, rows, columns_ref, one_ref, bias_ref, two_ref, out_bias_ref, noise_ref, terms
):
    block = rows * width
    group = noise_ref.shape[0]
    band = columns_ref.shape[0]
    lane = lax.broadcasted_iota(jnp.int32, (band, block), 1) % width
    out_lane = lax.broadcasted_iota(jnp.int32, (group, block), 1) % width
    terms[:, :width] = jnp.zeros((terms.shape[0], width), jnp.float32)
    terms[:, (height + 1) * width :] = jnp.zeros((terms.shape[0], width), jnp.float32)

    def hidden_step(step, carry):
        start = pl.multiple_of(step * block, block)
        parts = []
        for row_shift in range(3):
            here = columns_ref[:, pl.ds(pl.multiple_of(start + row_shift * width, width), block)]
            here = here.astype(jnp.float32)
            left = jnp.where(lane == 0, 0.0, pltpu.roll(here, 1, 1))
            right = jnp.where(lane == width - 1, 0.0, pltpu.roll(here, block - 1, 1))
            parts += [left, here, right]
        columns = jnp.concatenate([part.astype(jnp.bfloat16) for part in parts], axis=0)
        summed = jnp.dot(one_ref[...], columns, preferred_element_type=jnp.float32)
        hidden = jnp.maximum(summed + bias_ref[:, :1], 0.0) * bias_ref[:, 1:2]
        terms[:, pl.ds(pl.multiple_of(start + width, width), block)] = jnp.dot(
            two_ref[...], hidden.astype(jnp.bfloat16), preferred_element_type=jnp.float32
        )
        return carry

    lax.fori_loop(0, height // rows, hidden_step, 0)

    def sum_step(step, carry):
        start = pl.multiple_of(step * block, block)
        sums = []
        for column_shift in range(3):
            total = None
            for row_shift in range(3):
                first = (3 * row_shift + column_shift) * group
                piece = terms[
                    first : first + group,
                    pl.ds(pl.multiple_of(start + row_shift * width, width), block),
                ]
                total = piece if total is None else total + piece
            sums.append(total)
        left = jnp.where(out_lane == 0, 0.0, pltpu.roll(sums[0], 1, 1))
        right = jnp.where(out_lane == width - 1, 0.0, pltpu.roll(sums[2], block - 1, 1))
        noise_ref[:, pl.ds(start, block)] = left + sums[1] + right + out_bias_ref[:, :1]
        return carry

    lax.fori_loop(0, height // rows, sum_step, 0)


def denoise(widened, kernel_one, first_bias, kernel_two, second_bias, inside):
    channels, deep, height, width = widened.shape
    mid = deep - 2
    depth = deep - 4
    hid = first_bias.shape[0]
    band = -(-channels * deep // 16) * 16
    group = -(-channels * depth // 8) * 8
    columns = jnp.transpose(widened, (1, 0, 2, 3)).reshape(deep * channels, height * width)
    columns = jnp.pad(columns, ((0, band - deep * channels), (width, width)))
    taps = jnp.arange(3)
    place_one = (
        jnp.arange(deep)[None, :, None] == jnp.arange(mid)[:, None, None] + taps[None, None, :]
    ).astype(jnp.bfloat16)
    place_two = (
        jnp.arange(mid)[None, :, None] == jnp.arange(depth)[:, None, None] + taps[None, None, :]
    ).astype(jnp.bfloat16)
    one = jnp.einsum(
        "szd,dyxio->soyxzi",
        place_one,
        kernel_one.reshape(3, 3, 3, channels, hid),
        preferred_element_type=jnp.float32,
    ).astype(jnp.bfloat16)
    one = one.reshape(mid * hid, 9, deep * channels)
    one = jnp.pad(one, ((0, 0), (0, 0), (0, band - deep * channels))).reshape(mid * hid, 9 * band)
    two = jnp.einsum(
        "zsd,dyxho->yxzosh",
        place_two,
        kernel_two.reshape(3, 3, 3, hid, channels),
        preferred_element_type=jnp.float32,
    ).astype(jnp.bfloat16)
    two = two.reshape(9, depth * channels, mid * hid)
    two = jnp.pad(two, ((0, 0), (0, group - depth * channels), (0, 0))).reshape(9 * group, mid * hid)
    bias = jnp.stack([jnp.tile(first_bias, mid), jnp.repeat(inside.astype(jnp.float32), hid)], axis=1)
    out_bias = jnp.pad(jnp.tile(second_bias, depth), (0, group - depth * channels))[:, None]
    rows = math.gcd(8, height)
    noise = pl.pallas_call(
        functools.partial(conv_kernel, depth, height, width, rows),
        out_shape=jax.ShapeDtypeStruct((group, height * width), jnp.float32),
        in_specs=[pl.BlockSpec(memory_space=pltpu.VMEM)] * 5,
        out_specs=pl.BlockSpec(memory_space=pltpu.VMEM),
        scratch_shapes=[pltpu.VMEM((9 * group, (height + 2) * width), jnp.float32)],
        compiler_params=pltpu.CompilerParams(vmem_limit_bytes=32 * 1024 * 1024),
        name="denoise",
    )(columns, one, bias, two, out_bias)
    noise = noise[: depth * channels].reshape(depth, channels, height, width)
    return jnp.transpose(noise, (1, 0, 2, 3))


def scatter_kernel(bits, partial_ref, total_ref, *scratch):
    arrived, (send_sem, recv_sem) = scratch[:-2], scratch[-2:]
    me = lax.axis_index("slc")
    mine = [me // 2**bit % 2 for bit in range(bits)]
    partner = [me + (1 - 2 * mine[bit]) * 2**bit for bit in range(bits)]
    half = partial_ref.shape[-2] // 2
    orders = [list(range(bits)), [0, *range(2, bits), 1][:bits]]

    barrier = pltpu.get_barrier_semaphore()
    for bit in range(bits):
        pl.semaphore_signal(
            barrier, inc=1, device_id={"slc": partner[bit]}, device_id_type=pl.DeviceIdType.MESH
        )
    pl.semaphore_wait(barrier, bits)

    held = [partial_ref.at[..., pl.ds(chain * half, half), :] for chain in range(2)]
    left = [list(range(bits - 1, -1, -1)) for _ in range(2)]
    copies = [[], []]

    def part(chain, bit, choice):
        place = left[chain].index(bit)
        return held[chain].at[(slice(None),) * place + (choice,)]

    def send(chain, step):
        bit = orders[chain][step]
        copy = pltpu.make_async_remote_copy(
            src_ref=part(chain, bit, 1 - mine[bit]),
            dst_ref=arrived[chain * bits + step],
            send_sem=send_sem.at[chain, step],
            recv_sem=recv_sem.at[chain, step],
            device_id={"slc": partner[bit]},
            device_id_type=pl.DeviceIdType.MESH,
        )
        copy.start()
        copies[chain].append(copy)

    for chain in range(2):
        send(chain, 0)
    for step in range(bits):
        for chain in range(2):
            bit = orders[chain][step]
            landed = arrived[chain * bits + step]
            copies[chain][step].wait_recv()
            kept = part(chain, bit, mine[bit])[...].astype(jnp.float32)
            summed = kept + landed[...].astype(jnp.float32)
            if step == bits - 1:
                total_ref[chain * half : (chain + 1) * half, :] = summed
            else:
                landed[...] = summed.astype(landed.dtype)
                held[chain] = landed
                left[chain].remove(bit)
                send(chain, step + 1)
    for chain in range(2):
        for copy in copies[chain]:
            copy.wait_send()


def sum_scatter(partial):
    count, rows, width = partial.shape
    bits = count.bit_length() - 1
    landing = [
        pltpu.VMEM((2,) * (bits - 1 - step) + (rows // 2, width), partial.dtype)
        for _ in range(2)
        for step in range(bits)
    ]
    return pl.pallas_call(
        functools.partial(scatter_kernel, bits),
        out_shape=jax.ShapeDtypeStruct((rows, width), jnp.float32),
        in_specs=[pl.BlockSpec(memory_space=pltpu.VMEM)],
        out_specs=pl.BlockSpec(memory_space=pltpu.VMEM),
        scratch_shapes=landing
        + [pltpu.SemaphoreType.DMA((2, bits)), pltpu.SemaphoreType.DMA((2, bits))],
        compiler_params=pltpu.CompilerParams(
            collective_id=0, has_side_effects=True, vmem_limit_bytes=32 * 1024 * 1024
        ),
        name="sum_scatter",
    )(partial.reshape((2,) * bits + (rows, width)))


def gather_kernel(bits, block_ref, whole_ref, send_sem, recv_sem):
    me = lax.axis_index("slc")
    mine = [me // 2**bit % 2 for bit in range(bits)]
    partner = [me + (1 - 2 * mine[bit]) * 2**bit for bit in range(bits)]
    half = block_ref.shape[0] // 2
    orders = [list(range(bits)), [0, *range(2, bits), 1][:bits]]

    barrier = pltpu.get_barrier_semaphore()
    for bit in range(bits):
        pl.semaphore_signal(
            barrier, inc=1, device_id={"slc": partner[bit]}, device_id_type=pl.DeviceIdType.MESH
        )
    whole_ref[tuple(mine[::-1])] = block_ref[...]
    pl.semaphore_wait(barrier, bits)

    copies = [[], []]
    for step in range(bits):
        for chain in range(2):
            order = orders[chain][::-1]
            if step:
                copies[chain][-1].wait_recv()
            place = tuple(
                slice(None) if bit in order[:step] else mine[bit]
                for bit in range(bits - 1, -1, -1)
            )
            held = whole_ref.at[place + (pl.ds(chain * half, half),)]
            copy = pltpu.make_async_remote_copy(
                src_ref=held,
                dst_ref=held,
                send_sem=send_sem.at[chain, step],
                recv_sem=recv_sem.at[chain, step],
                device_id={"slc": partner[order[step]]},
                device_id_type=pl.DeviceIdType.MESH,
            )
            copy.start()
            copies[chain].append(copy)
    for chain in range(2):
        copies[chain][-1].wait_recv()
    for chain in range(2):
        for copy in copies[chain]:
            copy.wait_send()


def gather_blocks(block, count):
    rows, width = block.shape
    bits = count.bit_length() - 1
    whole = pl.pallas_call(
        functools.partial(gather_kernel, bits),
        out_shape=jax.ShapeDtypeStruct((2,) * bits + (rows, width), block.dtype),
        in_specs=[pl.BlockSpec(memory_space=pltpu.VMEM)],
        out_specs=pl.BlockSpec(memory_space=pltpu.VMEM),
        scratch_shapes=[pltpu.SemaphoreType.DMA((2, bits)), pltpu.SemaphoreType.DMA((2, bits))],
        compiler_params=pltpu.CompilerParams(
            collective_id=1, has_side_effects=True, vmem_limit_bytes=32 * 1024 * 1024
        ),
        cost_estimate=pl.CostEstimate(
            flops=0, transcendentals=0, bytes_accessed=24 * count * rows * width
        ),
        name="gather_blocks",
    )(block)
    return whole.reshape(count, rows, width)


def on_device(
    kspace, coil_maps, sample_mask, tap_order, first_kernel, first_bias, second_kernel, second_bias
):
    position = lax.axis_index("slc")
    slab_depth = coil_maps.shape[1]
    slices = kspace.shape[1]
    points = kspace.shape[3]
    table_cols = make_table(W, -1.0)
    table_rows = make_table(H, -1.0)
    table_depth = make_table(slices, -1.0)
    inverse_cols = make_table(W, 1.0)
    inverse_rows = make_table(H, 1.0)
    inverse_depth = make_table(slices, 1.0)
    point_rows = (position * points + jnp.arange(points, dtype=jnp.int32)) // W
    row_picker = (point_rows[None, :] == jnp.arange(H, dtype=jnp.int32)[:, None]).astype(
        jnp.bfloat16
    )
    sampled = jnp.einsum(
        "zch,hp->zcp",
        sample_mask.astype(jnp.bfloat16),
        row_picker,
        preferred_element_type=jnp.float32,
    )
    count = slices // slab_depth
    own_rows = points // W
    measured = kspace.reshape(2, slices, C, own_rows, W).astype(jnp.float32)
    sampled = sampled.reshape(slices, C, own_rows, W)
    map_real = coil_maps[0]
    map_imag = coil_maps[1]

    def adjoint(residual):
        depth_back = jnp.einsum(
            "pjcrx,pjqk->kqcrx", residual, inverse_depth, preferred_element_type=jnp.float32
        ).astype(jnp.bfloat16)
        slabs = lax.all_to_all(depth_back, "slc", split_axis=0, concat_axis=0, tiled=True)
        slabs = slabs.reshape(count, slab_depth, 2, C, own_rows, W)
        slabs = jnp.transpose(slabs, (2, 1, 3, 0, 4, 5)).reshape(2, slab_depth, C, H, W)
        upward = jnp.einsum(
            "pscjx,pjqk->qsckx", slabs, inverse_rows, preferred_element_type=jnp.float32
        ).astype(jnp.bfloat16)
        image_back = jnp.einsum(
            "pscyj,pjqk->qscyk", upward, inverse_cols, preferred_element_type=jnp.float32
        )
        real_sum = jnp.sum(map_real * image_back[0] + map_imag * image_back[1], axis=1)
        imag_sum = jnp.sum(map_real * image_back[1] - map_imag * image_back[0], axis=1)
        return jnp.stack([real_sum, imag_sum])

    def point_normal(before):
        image_real = before[0][:, None]
        image_imag = before[1][:, None]
        coil_image = jnp.stack(
            [
                map_real * image_real - map_imag * image_imag,
                map_real * image_imag + map_imag * image_real,
            ]
        ).astype(jnp.bfloat16)
        row_done = jnp.einsum(
            "pscyj,pjqk->qscyk", coil_image, table_cols, preferred_element_type=jnp.float32
        ).astype(jnp.bfloat16)
        plane = jnp.einsum(
            "pscjx,pjqk->qsckx", row_done, table_rows, preferred_element_type=jnp.float32
        ).astype(jnp.bfloat16)
        plane = plane.reshape(2, slab_depth, C, count, own_rows, W)
        plane = jnp.transpose(plane, (3, 1, 0, 2, 4, 5))
        pencil = lax.all_to_all(plane, "slc", split_axis=0, concat_axis=0, tiled=True)
        pencil = pencil.reshape(slices, 2, C, own_rows, W)
        spectrum = jnp.einsum(
            "jpcrx,pjqk->qkcrx", pencil, table_depth, preferred_element_type=jnp.float32
        )
        residual = (sampled[None] * (spectrum - measured)).astype(jnp.bfloat16)
        return adjoint(residual)

    def coil_normal(before):
        own_coils = C // count
        maps = maps_by_coil.reshape(count, own_coils, 2, slab_depth, H, W)
        own_real, own_imag = maps[:, :, 0], maps[:, :, 1]
        mask = lax.dynamic_slice_in_dim(sample_mask, position * own_coils, own_coils, axis=1)
        block = jnp.transpose(before, (1, 0, 2, 3)).astype(jnp.bfloat16)
        image = gather_blocks(block.reshape(slab_depth * 2 * H, W), count)
        image = image.reshape(count, slab_depth, 2, H, W)
        image_real = image[:, None, :, 0].astype(jnp.float32)
        image_imag = image[:, None, :, 1].astype(jnp.float32)
        coil_image = jnp.stack(
            [
                own_real * image_real - own_imag * image_imag,
                own_real * image_imag + own_imag * image_real,
            ]
        ).astype(jnp.bfloat16)
        row_done = jnp.einsum(
            "pncsyj,pjqk->qncsyk", coil_image, table_cols, preferred_element_type=jnp.float32
        ).astype(jnp.bfloat16)
        plane = jnp.einsum(
            "pncsjx,pjqk->qncskx", row_done, table_rows, preferred_element_type=jnp.float32
        ).astype(jnp.bfloat16)
        spectrum = jnp.einsum(
            "pncsyx,pnsqk->qkcyx",
            plane,
            table_depth.reshape(2, count, slab_depth, 2, slices),
            preferred_element_type=jnp.float32,
        )
        residual = (mask.astype(jnp.float32)[None, ..., None] * spectrum).astype(jnp.bfloat16)
        depth_back = jnp.einsum(
            "pjcyx,pjqns->qncsyx",
            residual,
            inverse_depth.reshape(2, slices, 2, count, slab_depth),
            preferred_element_type=jnp.float32,
        ).astype(jnp.bfloat16)
        upward = jnp.einsum(
            "pncsjx,pjqk->qncskx", depth_back, inverse_rows, preferred_element_type=jnp.float32
        ).astype(jnp.bfloat16)
        image_back = jnp.einsum(
            "pncsyj,pjqk->qncsyk", upward, inverse_cols, preferred_element_type=jnp.float32
        )
        real_sum = jnp.sum(own_real * image_back[0] + own_imag * image_back[1], axis=1)
        imag_sum = jnp.sum(own_real * image_back[1] - own_imag * image_back[0], axis=1)
        partial = jnp.stack([real_sum, imag_sum], axis=2).astype(jnp.bfloat16)
        total = sum_scatter(partial.reshape(count, slab_depth * 2 * H, W))
        return jnp.transpose(total.reshape(slab_depth, 2, H, W), (1, 0, 2, 3))

    kernel_one = tap_kernel(tap_order, first_kernel)
    kernel_two = tap_kernel(tap_order, second_kernel)
    by_coil = C % count == 0 and count > 1 and count & (count - 1) == 0
    data = (sampled[None] * measured).astype(jnp.bfloat16)
    if by_coil:
        maps_by_coil = jnp.transpose(coil_maps, (2, 0, 1, 3, 4))
        maps_by_coil = lax.all_to_all(
            maps_by_coil, "slc", split_axis=0, concat_axis=0, tiled=True
        )
    estimate = adjoint(data)
    before = estimate
    if by_coil:
        update = before + estimate - coil_normal(before)
    else:
        update = before - point_normal(before)
    field_low = update.astype(jnp.bfloat16)
    widened = padded_2(field_low, (("slc", 1),), 2)
    global_slice = position * slab_depth - 1 + jnp.arange(slab_depth + 2, dtype=jnp.int32)
    inside = (global_slice >= 0) & (global_slice < slices)
    estimate = update - denoise(widened, kernel_one, first_bias, kernel_two, second_bias, inside)
    dual_var = update - estimate
    return (estimate, dual_var)


def solution(mesh):
    placed = (
        P("grp", None, None, "slc"),
        P("grp", "slc", None, None, None),
        P("grp", None, None),
        P(),
        P(),
        P(),
        P(),
        P(),
    )
    return jax.shard_map(
        on_device,
        mesh=mesh,
        in_specs=placed,
        out_specs=(P("grp", "slc", None, None), P("grp", "slc", None, None)),
        check_vma=False,
    )
```

```python
import functools
import math

import jax
import jax.numpy as jnp
from jax import lax
from jax.experimental import pallas as pl
from jax.experimental.pallas import tpu as pltpu
from jax.sharding import PartitionSpec as P

C = 16
H = 128
W = 128


def padded_2(cells, sides, width):
    for axis, dim in sides:
        count = lax.axis_size(axis)
        ends = count - 1
        head = lax.slice_in_dim(cells, 0, width, axis=dim)
        tail = lax.slice_in_dim(cells, cells.shape[dim] - width, cells.shape[dim], axis=dim)
        cells = jnp.concatenate(
            [
                lax.ppermute(tail, axis, [(i, (i + 1) % count) for i in range(ends)]),
                cells,
                lax.ppermute(head, axis, [((i + 1) % count, i) for i in range(ends)]),
            ],
            axis=dim,
        )
    return cells


def make_table(length, direction):
    positions = jnp.arange(length, dtype=jnp.int32)
    product = positions[:, None] * positions[None, :] % length
    angles = 2.0 * math.pi / length * product.astype(jnp.float32)
    norm_scale = 1.0 / math.sqrt(length)
    real_part = (jnp.cos(angles) * norm_scale).astype(jnp.bfloat16)
    imaginary = (direction * jnp.sin(angles) * norm_scale).astype(jnp.bfloat16)
    real_t = jnp.transpose(real_part)
    imag_t = jnp.transpose(imaginary)
    upper = jnp.stack([real_t, imag_t], axis=1)
    lower = jnp.stack([-imag_t, real_t], axis=1)
    return jnp.stack([upper, lower])


def tap_kernel(tap_order, stored):
    chosen = (tap_order[None, :] == jnp.arange(27, dtype=jnp.int32)[:, None]).astype(jnp.bfloat16)
    return jnp.einsum("tq,qio->tio", chosen, stored, preferred_element_type=jnp.float32).astype(
        jnp.bfloat16
    )


def conv_kernel(
    depth, height, width, rows, columns_ref, one_ref, bias_ref, two_ref, out_bias_ref, noise_ref, terms
):
    block = rows * width
    group = noise_ref.shape[0]
    band = columns_ref.shape[0]
    lane = lax.broadcasted_iota(jnp.int32, (band, block + 2 * width), 1) % width
    out_lane = lax.broadcasted_iota(jnp.int32, (group, block), 1) % width
    terms[:, :width] = jnp.zeros((terms.shape[0], width), jnp.float32)
    terms[:, (height + 1) * width :] = jnp.zeros((terms.shape[0], width), jnp.float32)

    def hidden_step(step, carry):
        start = pl.multiple_of(step * block, block)
        here = columns_ref[:, pl.ds(start, block + 2 * width)]
        wide = here.astype(jnp.float32)
        span = block + 2 * width
        left = jnp.where(lane == 0, 0.0, pltpu.roll(wide, 1, 1)).astype(jnp.bfloat16)
        right = jnp.where(lane == width - 1, 0.0, pltpu.roll(wide, span - 1, 1))
        shifted = jnp.concatenate([left, here, right.astype(jnp.bfloat16)], axis=0)
        columns = jnp.concatenate(
            [shifted[:, row * width : row * width + block] for row in range(3)], axis=0
        )
        summed = jnp.dot(one_ref[...], columns, preferred_element_type=jnp.float32)
        hidden = jnp.maximum(summed + bias_ref[:, :1], 0.0)
        terms[:, pl.ds(pl.multiple_of(start + width, width), block)] = jnp.dot(
            two_ref[...], hidden.astype(jnp.bfloat16), preferred_element_type=jnp.float32
        )
        return carry

    lax.fori_loop(0, height // rows, hidden_step, 0)

    def sum_step(step, carry):
        start = pl.multiple_of(step * block, block)
        sums = []
        for column_shift in range(3):
            total = None
            for row_shift in range(3):
                first = (3 * row_shift + column_shift) * group
                piece = terms[
                    first : first + group,
                    pl.ds(pl.multiple_of(start + row_shift * width, width), block),
                ]
                total = piece if total is None else total + piece
            sums.append(total)
        left = jnp.where(out_lane == 0, 0.0, pltpu.roll(sums[0], 1, 1))
        right = jnp.where(out_lane == width - 1, 0.0, pltpu.roll(sums[2], block - 1, 1))
        noise_ref[:, pl.ds(start, block)] = left + sums[1] + right + out_bias_ref[:, :1]
        return carry

    lax.fori_loop(0, height // rows, sum_step, 0)


def denoiser_weights(depth, kernel_one, first_bias, kernel_two, second_bias, inside):
    channels, hid = kernel_one.shape[1:]
    deep = depth + 4
    mid = depth + 2
    band = -(-channels * deep // 16) * 16
    group = -(-channels * depth // 8) * 8
    taps = jnp.arange(3)
    place_one = (
        jnp.arange(deep)[None, :, None] == jnp.arange(mid)[:, None, None] + taps[None, None, :]
    ).astype(jnp.bfloat16)
    place_two = (
        jnp.arange(mid)[None, :, None] == jnp.arange(depth)[:, None, None] + taps[None, None, :]
    ).astype(jnp.bfloat16)
    one = jnp.einsum(
        "szd,dyxio->soyxzi",
        place_one,
        kernel_one.reshape(3, 3, 3, channels, hid),
        preferred_element_type=jnp.float32,
    ).astype(jnp.bfloat16)
    one = one.reshape(mid * hid, 9, deep * channels)
    one = jnp.pad(one, ((0, 0), (0, 0), (0, band - deep * channels))).reshape(mid * hid, 9 * band)
    two = jnp.einsum(
        "zsd,dyxho->yxzosh",
        place_two,
        kernel_two.reshape(3, 3, 3, hid, channels),
        preferred_element_type=jnp.float32,
    ).astype(jnp.bfloat16)
    two = two.reshape(9, depth * channels, mid * hid)
    two = two * jnp.repeat(inside.astype(jnp.bfloat16), hid)
    two = jnp.pad(two, ((0, 0), (0, group - depth * channels), (0, 0))).reshape(9 * group, mid * hid)
    bias = jnp.tile(first_bias, mid)[:, None]
    out_bias = jnp.pad(jnp.tile(second_bias, depth), (0, group - depth * channels))[:, None]
    return one, bias, two, out_bias


def denoise(widened, one, bias, two, out_bias):
    channels, deep, height, width = widened.shape
    depth = deep - 4
    group = out_bias.shape[0]
    band = one.shape[1] // 9
    columns = jnp.transpose(widened, (1, 0, 2, 3)).reshape(deep * channels, height * width)
    columns = jnp.pad(columns, ((0, band - deep * channels), (width, width)))
    rows = math.gcd(8, height)
    noise = pl.pallas_call(
        functools.partial(conv_kernel, depth, height, width, rows),
        out_shape=jax.ShapeDtypeStruct((group, height * width), jnp.float32),
        in_specs=[pl.BlockSpec(memory_space=pltpu.VMEM)] * 5,
        out_specs=pl.BlockSpec(memory_space=pltpu.VMEM),
        scratch_shapes=[pltpu.VMEM((9 * group, (height + 2) * width), jnp.float32)],
        compiler_params=pltpu.CompilerParams(vmem_limit_bytes=32 * 1024 * 1024),
        name="denoise",
    )(columns, one, bias, two, out_bias)
    noise = noise[: depth * channels].reshape(depth, channels, height, width)
    return jnp.transpose(noise, (1, 0, 2, 3))


def scatter_kernel(bits, partial_ref, total_ref, *scratch):
    arrived, (send_sem, recv_sem) = scratch[:-2], scratch[-2:]
    me = lax.axis_index("slc")
    mine = [me // 2**bit % 2 for bit in range(bits)]
    partner = [me + (1 - 2 * mine[bit]) * 2**bit for bit in range(bits)]
    half = partial_ref.shape[-2] // 2
    orders = [list(range(bits)), [0, *range(2, bits), 1][:bits]]

    barrier = pltpu.get_barrier_semaphore()
    for bit in range(bits):
        pl.semaphore_signal(
            barrier, inc=1, device_id={"slc": partner[bit]}, device_id_type=pl.DeviceIdType.MESH
        )
    pl.semaphore_wait(barrier, bits)

    held = [partial_ref.at[..., pl.ds(chain * half, half), :] for chain in range(2)]
    left = [list(range(bits - 1, -1, -1)) for _ in range(2)]
    copies = [[], []]

    def part(chain, bit, choice):
        place = left[chain].index(bit)
        return held[chain].at[(slice(None),) * place + (choice,)]

    def send(chain, step):
        bit = orders[chain][step]
        copy = pltpu.make_async_remote_copy(
            src_ref=part(chain, bit, 1 - mine[bit]),
            dst_ref=arrived[chain * bits + step],
            send_sem=send_sem.at[chain, step],
            recv_sem=recv_sem.at[chain, step],
            device_id={"slc": partner[bit]},
            device_id_type=pl.DeviceIdType.MESH,
        )
        copy.start()
        copies[chain].append(copy)

    for chain in range(2):
        send(chain, 0)
    for step in range(bits):
        for chain in range(2):
            bit = orders[chain][step]
            landed = arrived[chain * bits + step]
            copies[chain][step].wait_recv()
            kept = part(chain, bit, mine[bit])[...].astype(jnp.float32)
            summed = kept + landed[...].astype(jnp.float32)
            if step == bits - 1:
                total_ref[chain * half : (chain + 1) * half, :] = summed
            else:
                landed[...] = summed.astype(landed.dtype)
                held[chain] = landed
                left[chain].remove(bit)
                send(chain, step + 1)
    for chain in range(2):
        for copy in copies[chain]:
            copy.wait_send()


def sum_scatter(partial):
    count, rows, width = partial.shape
    bits = count.bit_length() - 1
    landing = [
        pltpu.VMEM((2,) * (bits - 1 - step) + (rows // 2, width), partial.dtype)
        for _ in range(2)
        for step in range(bits)
    ]
    return pl.pallas_call(
        functools.partial(scatter_kernel, bits),
        out_shape=jax.ShapeDtypeStruct((rows, width), jnp.float32),
        in_specs=[pl.BlockSpec(memory_space=pltpu.VMEM)],
        out_specs=pl.BlockSpec(memory_space=pltpu.VMEM),
        scratch_shapes=landing
        + [pltpu.SemaphoreType.DMA((2, bits)), pltpu.SemaphoreType.DMA((2, bits))],
        compiler_params=pltpu.CompilerParams(
            collective_id=0, has_side_effects=True, vmem_limit_bytes=32 * 1024 * 1024
        ),
        name="sum_scatter",
    )(partial.reshape((2,) * bits + (rows, width)))


def gather_kernel(bits, block_ref, whole_ref, send_sem, recv_sem):
    me = lax.axis_index("slc")
    mine = [me // 2**bit % 2 for bit in range(bits)]
    partner = [me + (1 - 2 * mine[bit]) * 2**bit for bit in range(bits)]
    half = block_ref.shape[0] // 2
    orders = [list(range(bits)), [0, *range(2, bits), 1][:bits]]

    barrier = pltpu.get_barrier_semaphore()
    for bit in range(bits):
        pl.semaphore_signal(
            barrier, inc=1, device_id={"slc": partner[bit]}, device_id_type=pl.DeviceIdType.MESH
        )
    whole_ref[tuple(mine[::-1])] = block_ref[...]
    pl.semaphore_wait(barrier, bits)

    copies = [[], []]
    for step in range(bits):
        for chain in range(2):
            order = orders[chain][::-1]
            if step:
                copies[chain][-1].wait_recv()
            place = tuple(
                slice(None) if bit in order[:step] else mine[bit]
                for bit in range(bits - 1, -1, -1)
            )
            held = whole_ref.at[place + (pl.ds(chain * half, half),)]
            copy = pltpu.make_async_remote_copy(
                src_ref=held,
                dst_ref=held,
                send_sem=send_sem.at[chain, step],
                recv_sem=recv_sem.at[chain, step],
                device_id={"slc": partner[order[step]]},
                device_id_type=pl.DeviceIdType.MESH,
            )
            copy.start()
            copies[chain].append(copy)
    for chain in range(2):
        copies[chain][-1].wait_recv()
    for chain in range(2):
        for copy in copies[chain]:
            copy.wait_send()


def gather_blocks(block, count):
    rows, width = block.shape
    bits = count.bit_length() - 1
    whole = pl.pallas_call(
        functools.partial(gather_kernel, bits),
        out_shape=jax.ShapeDtypeStruct((2,) * bits + (rows, width), block.dtype),
        in_specs=[pl.BlockSpec(memory_space=pltpu.VMEM)],
        out_specs=pl.BlockSpec(memory_space=pltpu.VMEM),
        scratch_shapes=[pltpu.SemaphoreType.DMA((2, bits)), pltpu.SemaphoreType.DMA((2, bits))],
        compiler_params=pltpu.CompilerParams(
            collective_id=1, has_side_effects=True, vmem_limit_bytes=32 * 1024 * 1024
        ),
        cost_estimate=pl.CostEstimate(
            flops=0, transcendentals=0, bytes_accessed=24 * count * rows * width
        ),
        name="gather_blocks",
    )(block)
    return whole.reshape(count, rows, width)


def on_device(
    kspace, coil_maps, sample_mask, tap_order, first_kernel, first_bias, second_kernel, second_bias
):
    position = lax.axis_index("slc")
    slab_depth = coil_maps.shape[1]
    slices = kspace.shape[1]
    points = kspace.shape[3]
    table_cols = make_table(W, -1.0)
    table_rows = make_table(H, -1.0)
    table_depth = make_table(slices, -1.0)
    inverse_cols = make_table(W, 1.0)
    inverse_rows = make_table(H, 1.0)
    inverse_depth = make_table(slices, 1.0)
    point_rows = (position * points + jnp.arange(points, dtype=jnp.int32)) // W
    row_picker = (point_rows[None, :] == jnp.arange(H, dtype=jnp.int32)[:, None]).astype(
        jnp.bfloat16
    )
    sampled = jnp.einsum(
        "zch,hp->zcp",
        sample_mask.astype(jnp.bfloat16),
        row_picker,
        preferred_element_type=jnp.float32,
    )
    count = slices // slab_depth
    own_rows = points // W
    measured = kspace.reshape(2, slices, C, own_rows, W).astype(jnp.float32)
    sampled = sampled.reshape(slices, C, own_rows, W)
    map_real = coil_maps[0]
    map_imag = coil_maps[1]

    def adjoint(residual, ready=None):
        depth_back = jnp.einsum(
            "pjcrx,pjqk->kqcrx", residual, inverse_depth, preferred_element_type=jnp.float32
        ).astype(jnp.bfloat16)
        slabs = lax.all_to_all(depth_back, "slc", split_axis=0, concat_axis=0, tiled=True)
        if ready is not None:
            slabs, ready = lax.optimization_barrier((slabs, ready))
        slabs = slabs.reshape(count, slab_depth, 2, C, own_rows, W)
        slabs = jnp.transpose(slabs, (2, 1, 3, 0, 4, 5)).reshape(2, slab_depth, C, H, W)
        upward = jnp.einsum(
            "pscjx,pjqk->qsckx", slabs, inverse_rows, preferred_element_type=jnp.float32
        ).astype(jnp.bfloat16)
        image_back = jnp.einsum(
            "pscyj,pjqk->qscyk", upward, inverse_cols, preferred_element_type=jnp.float32
        )
        real_sum = jnp.sum(map_real * image_back[0] + map_imag * image_back[1], axis=1)
        imag_sum = jnp.sum(map_real * image_back[1] - map_imag * image_back[0], axis=1)
        combined = jnp.stack([real_sum, imag_sum])
        return combined if ready is None else (combined, ready)

    def point_normal(before):
        image_real = before[0][:, None]
        image_imag = before[1][:, None]
        coil_image = jnp.stack(
            [
                map_real * image_real - map_imag * image_imag,
                map_real * image_imag + map_imag * image_real,
            ]
        ).astype(jnp.bfloat16)
        row_done = jnp.einsum(
            "pscyj,pjqk->qscyk", coil_image, table_cols, preferred_element_type=jnp.float32
        ).astype(jnp.bfloat16)
        plane = jnp.einsum(
            "pscjx,pjqk->qsckx", row_done, table_rows, preferred_element_type=jnp.float32
        ).astype(jnp.bfloat16)
        plane = plane.reshape(2, slab_depth, C, count, own_rows, W)
        plane = jnp.transpose(plane, (3, 1, 0, 2, 4, 5))
        pencil = lax.all_to_all(plane, "slc", split_axis=0, concat_axis=0, tiled=True)
        pencil = pencil.reshape(slices, 2, C, own_rows, W)
        spectrum = jnp.einsum(
            "jpcrx,pjqk->qkcrx", pencil, table_depth, preferred_element_type=jnp.float32
        )
        residual = (sampled[None] * (spectrum - measured)).astype(jnp.bfloat16)
        return adjoint(residual)

    def coil_normal(before):
        own_coils = C // count
        maps = maps_by_coil.reshape(count, own_coils, 2, slab_depth, H, W)
        own_real, own_imag = maps[:, :, 0], maps[:, :, 1]
        block = jnp.transpose(before, (1, 0, 2, 3)).astype(jnp.bfloat16)
        image = gather_blocks(block.reshape(slab_depth * 2 * H, W), count)
        image = image.reshape(count, slab_depth, 2, H, W)
        image_real = image[:, None, :, 0].astype(jnp.float32)
        image_imag = image[:, None, :, 1].astype(jnp.float32)
        coil_image = jnp.stack(
            [
                own_real * image_real - own_imag * image_imag,
                own_real * image_imag + own_imag * image_real,
            ]
        ).astype(jnp.bfloat16)
        row_done = jnp.einsum(
            "pncsyj,pjqk->qncsyk", coil_image, table_cols, preferred_element_type=jnp.float32
        ).astype(jnp.bfloat16)
        plane = jnp.einsum(
            "pncsjx,pjqk->qncskx", row_done, table_rows, preferred_element_type=jnp.float32
        ).astype(jnp.bfloat16)
        spectrum = jnp.einsum(
            "pncsyx,pnsqk->qkcyx",
            plane,
            table_depth.reshape(2, count, slab_depth, 2, slices),
            preferred_element_type=jnp.float32,
        )
        residual = (own_mask[None, ..., None] * spectrum).astype(jnp.bfloat16)
        depth_back = jnp.einsum(
            "pjcyx,pjqns->qncsyx",
            residual,
            inverse_depth.reshape(2, slices, 2, count, slab_depth),
            preferred_element_type=jnp.float32,
        ).astype(jnp.bfloat16)
        upward = jnp.einsum(
            "pncsjx,pjqk->qncskx", depth_back, inverse_rows, preferred_element_type=jnp.float32
        ).astype(jnp.bfloat16)
        image_back = jnp.einsum(
            "pncsyj,pjqk->qncsyk", upward, inverse_cols, preferred_element_type=jnp.float32
        )
        real_sum = jnp.sum(own_real * image_back[0] + own_imag * image_back[1], axis=1)
        imag_sum = jnp.sum(own_real * image_back[1] - own_imag * image_back[0], axis=1)
        partial = jnp.stack([real_sum, imag_sum], axis=2).astype(jnp.bfloat16)
        total = sum_scatter(partial.reshape(count, slab_depth * 2 * H, W))
        return jnp.transpose(total.reshape(slab_depth, 2, H, W), (1, 0, 2, 3))

    kernel_one = tap_kernel(tap_order, first_kernel)
    kernel_two = tap_kernel(tap_order, second_kernel)
    global_slice = position * slab_depth - 1 + jnp.arange(slab_depth + 2, dtype=jnp.int32)
    inside = (global_slice >= 0) & (global_slice < slices)
    weights = denoiser_weights(
        slab_depth, kernel_one, first_bias, kernel_two, second_bias, inside
    )
    by_coil = C % count == 0 and count > 1 and count & (count - 1) == 0
    data = (sampled[None] * measured).astype(jnp.bfloat16)
    if by_coil:
        maps_by_coil = jnp.transpose(coil_maps, (2, 0, 1, 3, 4))
        maps_by_coil = lax.all_to_all(
            maps_by_coil, "slc", split_axis=0, concat_axis=0, tiled=True
        )
        own_mask = lax.dynamic_slice_in_dim(
            sample_mask, position * (C // count), C // count, axis=1
        ).astype(jnp.float32)
        ready = (own_mask, weights)
    else:
        ready = (weights,)
    estimate, ready = adjoint(data, ready)
    weights = ready[-1]
    if by_coil:
        own_mask = ready[0]
    before = estimate
    if by_coil:
        update = before + estimate - coil_normal(before)
    else:
        update = before - point_normal(before)
    field_low = update.astype(jnp.bfloat16)
    widened = padded_2(field_low, (("slc", 1),), 2)
    estimate = update - denoise(widened, *weights)
    dual_var = update - estimate
    return (estimate, dual_var)


def solution(mesh):
    placed = (
        P("grp", None, None, "slc"),
        P("grp", "slc", None, None, None),
        P("grp", None, None),
        P(),
        P(),
        P(),
        P(),
        P(),
    )
    return jax.shard_map(
        on_device,
        mesh=mesh,
        in_specs=placed,
        out_specs=(P("grp", "slc", None, None), P("grp", "slc", None, None)),
        check_vma=False,
    )
```

```python
import functools
import math

import jax
import jax.numpy as jnp
from jax import lax
from jax.experimental import pallas as pl
from jax.experimental.pallas import tpu as pltpu
from jax.sharding import PartitionSpec as P

C = 16
H = 128
W = 128


def padded_2(cells, sides, width):
    for axis, dim in sides:
        count = lax.axis_size(axis)
        ends = count - 1
        head = lax.slice_in_dim(cells, 0, width, axis=dim)
        tail = lax.slice_in_dim(cells, cells.shape[dim] - width, cells.shape[dim], axis=dim)
        cells = jnp.concatenate(
            [
                lax.ppermute(tail, axis, [(i, (i + 1) % count) for i in range(ends)]),
                cells,
                lax.ppermute(head, axis, [((i + 1) % count, i) for i in range(ends)]),
            ],
            axis=dim,
        )
    return cells


def make_table(length, direction):
    positions = jnp.arange(length, dtype=jnp.int32)
    product = positions[:, None] * positions[None, :] % length
    angles = 2.0 * math.pi / length * product.astype(jnp.float32)
    norm_scale = 1.0 / math.sqrt(length)
    real_part = (jnp.cos(angles) * norm_scale).astype(jnp.bfloat16)
    imaginary = (direction * jnp.sin(angles) * norm_scale).astype(jnp.bfloat16)
    real_t = jnp.transpose(real_part)
    imag_t = jnp.transpose(imaginary)
    upper = jnp.stack([real_t, imag_t], axis=1)
    lower = jnp.stack([-imag_t, real_t], axis=1)
    return jnp.stack([upper, lower])


def tap_kernel(tap_order, stored):
    chosen = (tap_order[None, :] == jnp.arange(27, dtype=jnp.int32)[:, None]).astype(jnp.bfloat16)
    return jnp.einsum("tq,qio->tio", chosen, stored, preferred_element_type=jnp.float32).astype(
        jnp.bfloat16
    )


def conv_kernel(
    depth, height, width, rows, columns_ref, one_ref, bias_ref, two_ref, out_bias_ref, noise_ref, terms
):
    block = rows * width
    group = noise_ref.shape[0]
    band = columns_ref.shape[0]
    lane = lax.broadcasted_iota(jnp.int32, (band, block + 2 * width), 1) % width
    out_lane = lax.broadcasted_iota(jnp.int32, (group, block), 1) % width
    terms[:, :width] = jnp.zeros((terms.shape[0], width), jnp.float32)
    terms[:, (height + 1) * width :] = jnp.zeros((terms.shape[0], width), jnp.float32)

    def hidden_step(step, carry):
        start = pl.multiple_of(step * block, block)
        here = columns_ref[:, pl.ds(start, block + 2 * width)]
        wide = here.astype(jnp.float32)
        span = block + 2 * width
        left = jnp.where(lane == 0, 0.0, pltpu.roll(wide, 1, 1)).astype(jnp.bfloat16)
        right = jnp.where(lane == width - 1, 0.0, pltpu.roll(wide, span - 1, 1))
        shifted = jnp.concatenate([left, here, right.astype(jnp.bfloat16)], axis=0)
        columns = jnp.concatenate(
            [shifted[:, row * width : row * width + block] for row in range(3)], axis=0
        )
        summed = jnp.dot(one_ref[...], columns, preferred_element_type=jnp.float32)
        hidden = jnp.maximum(summed + bias_ref[:, :1], 0.0)
        terms[:, pl.ds(pl.multiple_of(start + width, width), block)] = jnp.dot(
            two_ref[...], hidden.astype(jnp.bfloat16), preferred_element_type=jnp.float32
        )
        return carry

    lax.fori_loop(0, height // rows, hidden_step, 0)

    def sum_step(step, carry):
        start = pl.multiple_of(step * block, block)
        sums = []
        for column_shift in range(3):
            total = None
            for row_shift in range(3):
                first = (3 * row_shift + column_shift) * group
                piece = terms[
                    first : first + group,
                    pl.ds(pl.multiple_of(start + row_shift * width, width), block),
                ]
                total = piece if total is None else total + piece
            sums.append(total)
        left = jnp.where(out_lane == 0, 0.0, pltpu.roll(sums[0], 1, 1))
        right = jnp.where(out_lane == width - 1, 0.0, pltpu.roll(sums[2], block - 1, 1))
        noise_ref[:, pl.ds(start, block)] = left + sums[1] + right + out_bias_ref[:, :1]
        return carry

    lax.fori_loop(0, height // rows, sum_step, 0)


def denoiser_weights(depth, kernel_one, first_bias, kernel_two, second_bias, inside):
    channels, hid = kernel_one.shape[1:]
    deep = depth + 4
    mid = depth + 2
    band = -(-channels * deep // 16) * 16
    group = -(-channels * depth // 8) * 8
    taps = jnp.arange(3)
    place_one = (
        jnp.arange(deep)[None, :, None] == jnp.arange(mid)[:, None, None] + taps[None, None, :]
    ).astype(jnp.bfloat16)
    place_two = (
        jnp.arange(mid)[None, :, None] == jnp.arange(depth)[:, None, None] + taps[None, None, :]
    ).astype(jnp.bfloat16)
    one = jnp.einsum(
        "szd,dyxio->soyxzi",
        place_one,
        kernel_one.reshape(3, 3, 3, channels, hid),
        preferred_element_type=jnp.float32,
    ).astype(jnp.bfloat16)
    one = one.reshape(mid * hid, 9, deep * channels)
    one = jnp.pad(one, ((0, 0), (0, 0), (0, band - deep * channels))).reshape(mid * hid, 9 * band)
    two = jnp.einsum(
        "zsd,dyxho->yxzosh",
        place_two,
        kernel_two.reshape(3, 3, 3, hid, channels),
        preferred_element_type=jnp.float32,
    ).astype(jnp.bfloat16)
    two = two.reshape(9, depth * channels, mid * hid)
    two = two * jnp.repeat(inside.astype(jnp.bfloat16), hid)
    two = jnp.pad(two, ((0, 0), (0, group - depth * channels), (0, 0))).reshape(9 * group, mid * hid)
    bias = jnp.tile(first_bias, mid)[:, None]
    out_bias = jnp.pad(jnp.tile(second_bias, depth), (0, group - depth * channels))[:, None]
    return one, bias, two, out_bias


def denoise(widened, one, bias, two, out_bias):
    deep, channels, height, width = widened.shape
    depth = deep - 4
    group = out_bias.shape[0]
    band = one.shape[1] // 9
    columns = widened.reshape(deep * channels, height * width)
    columns = jnp.pad(columns, ((0, band - deep * channels), (width, width)))
    rows = math.gcd(8, height)
    noise = pl.pallas_call(
        functools.partial(conv_kernel, depth, height, width, rows),
        out_shape=jax.ShapeDtypeStruct((group, height * width), jnp.float32),
        in_specs=[pl.BlockSpec(memory_space=pltpu.VMEM)] * 5,
        out_specs=pl.BlockSpec(memory_space=pltpu.VMEM),
        scratch_shapes=[pltpu.VMEM((9 * group, (height + 2) * width), jnp.float32)],
        compiler_params=pltpu.CompilerParams(vmem_limit_bytes=32 * 1024 * 1024),
        name="denoise",
    )(columns, one, bias, two, out_bias)
    noise = noise[: depth * channels].reshape(depth, channels, height, width)
    return jnp.transpose(noise, (1, 0, 2, 3))


def scatter_kernel(bits, partial_ref, base_ref, total_ref, wide_ref, *scratch):
    arrived, (send_sem, recv_sem, edge_send, edge_recv) = scratch[:-4], scratch[-4:]
    me = lax.axis_index("slc")
    mine = [me // 2**bit % 2 for bit in range(bits)]
    partner = [me + (1 - 2 * mine[bit]) * 2**bit for bit in range(bits)]
    half = partial_ref.shape[-2] // 2
    orders = [list(range(bits)), [0, *range(2, bits), 1][:bits]]

    count = 2**bits
    around = [(me + 1) % count, (me + count - 1) % count]

    barrier = pltpu.get_barrier_semaphore()
    for other in partner + around:
        pl.semaphore_signal(
            barrier, inc=1, device_id={"slc": other}, device_id_type=pl.DeviceIdType.MESH
        )
    pl.semaphore_wait(barrier, bits + 2)

    held = [partial_ref.at[..., pl.ds(chain * half, half), :] for chain in range(2)]
    left = [list(range(bits - 1, -1, -1)) for _ in range(2)]
    copies = [[], []]

    def part(chain, bit, choice):
        place = left[chain].index(bit)
        return held[chain].at[(slice(None),) * place + (choice,)]

    def send(chain, step):
        bit = orders[chain][step]
        copy = pltpu.make_async_remote_copy(
            src_ref=part(chain, bit, 1 - mine[bit]),
            dst_ref=arrived[chain * bits + step],
            send_sem=send_sem.at[chain, step],
            recv_sem=recv_sem.at[chain, step],
            device_id={"slc": partner[bit]},
            device_id_type=pl.DeviceIdType.MESH,
        )
        copy.start()
        copies[chain].append(copy)

    for chain in range(2):
        send(chain, 0)
    for step in range(bits):
        for chain in range(2):
            bit = orders[chain][step]
            landed = arrived[chain * bits + step]
            copies[chain][step].wait_recv()
            kept = part(chain, bit, mine[bit])[...].astype(jnp.float32)
            summed = kept + landed[...].astype(jnp.float32)
            if step == bits - 1:
                rows = slice(chain * half, (chain + 1) * half)
                update = base_ref[rows, :] - summed
                total_ref[rows, :] = update
                wide_ref[1, rows, :] = update.astype(wide_ref.dtype)
            else:
                landed[...] = summed.astype(landed.dtype)
                held[chain] = landed
                left[chain].remove(bit)
                send(chain, step + 1)
    edges = []
    for side in range(2):
        copy = pltpu.make_async_remote_copy(
            src_ref=wide_ref.at[1],
            dst_ref=wide_ref.at[2 * side],
            send_sem=edge_send.at[side],
            recv_sem=edge_recv.at[side],
            device_id={"slc": around[side]},
            device_id_type=pl.DeviceIdType.MESH,
        )
        copy.start()
        edges.append(copy)
    for chain in range(2):
        for copy in copies[chain]:
            copy.wait_send()
    for copy in edges:
        copy.wait_recv()
    for side, present in ((0, me > 0), (2, me < count - 1)):
        wide_ref[side] = wide_ref[side] * present.astype(jnp.float32).astype(wide_ref.dtype)
    for copy in edges:
        copy.wait_send()


def sum_scatter(partial, base):
    count, rows, width = partial.shape
    bits = count.bit_length() - 1
    landing = [
        pltpu.VMEM((2,) * (bits - 1 - step) + (rows // 2, width), partial.dtype)
        for _ in range(2)
        for step in range(bits)
    ]
    return pl.pallas_call(
        functools.partial(scatter_kernel, bits),
        out_shape=[
            jax.ShapeDtypeStruct((rows, width), jnp.float32),
            jax.ShapeDtypeStruct((3, rows, width), partial.dtype),
        ],
        in_specs=[pl.BlockSpec(memory_space=pltpu.VMEM)] * 2,
        out_specs=[pl.BlockSpec(memory_space=pltpu.VMEM)] * 2,
        scratch_shapes=landing
        + [pltpu.SemaphoreType.DMA((2, bits))] * 2
        + [pltpu.SemaphoreType.DMA((2,))] * 2,
        compiler_params=pltpu.CompilerParams(
            collective_id=0, has_side_effects=True, vmem_limit_bytes=32 * 1024 * 1024
        ),
        name="sum_scatter",
    )(partial.reshape((2,) * bits + (rows, width)), base)


def gather_kernel(bits, block_ref, whole_ref, send_sem, recv_sem):
    me = lax.axis_index("slc")
    mine = [me // 2**bit % 2 for bit in range(bits)]
    partner = [me + (1 - 2 * mine[bit]) * 2**bit for bit in range(bits)]
    half = block_ref.shape[0] // 2
    orders = [list(range(bits)), [0, *range(2, bits), 1][:bits]]

    barrier = pltpu.get_barrier_semaphore()
    for bit in range(bits):
        pl.semaphore_signal(
            barrier, inc=1, device_id={"slc": partner[bit]}, device_id_type=pl.DeviceIdType.MESH
        )
    whole_ref[tuple(mine[::-1])] = block_ref[...]
    pl.semaphore_wait(barrier, bits)

    copies = [[], []]
    for step in range(bits):
        for chain in range(2):
            order = orders[chain][::-1]
            if step:
                copies[chain][-1].wait_recv()
            place = tuple(
                slice(None) if bit in order[:step] else mine[bit]
                for bit in range(bits - 1, -1, -1)
            )
            held = whole_ref.at[place + (pl.ds(chain * half, half),)]
            copy = pltpu.make_async_remote_copy(
                src_ref=held,
                dst_ref=held,
                send_sem=send_sem.at[chain, step],
                recv_sem=recv_sem.at[chain, step],
                device_id={"slc": partner[order[step]]},
                device_id_type=pl.DeviceIdType.MESH,
            )
            copy.start()
            copies[chain].append(copy)
    for chain in range(2):
        copies[chain][-1].wait_recv()
    for chain in range(2):
        for copy in copies[chain]:
            copy.wait_send()


def gather_blocks(block, count):
    rows, width = block.shape
    bits = count.bit_length() - 1
    whole = pl.pallas_call(
        functools.partial(gather_kernel, bits),
        out_shape=jax.ShapeDtypeStruct((2,) * bits + (rows, width), block.dtype),
        in_specs=[pl.BlockSpec(memory_space=pltpu.VMEM)],
        out_specs=pl.BlockSpec(memory_space=pltpu.VMEM),
        scratch_shapes=[pltpu.SemaphoreType.DMA((2, bits)), pltpu.SemaphoreType.DMA((2, bits))],
        compiler_params=pltpu.CompilerParams(
            collective_id=1, has_side_effects=True, vmem_limit_bytes=32 * 1024 * 1024
        ),
        cost_estimate=pl.CostEstimate(
            flops=0, transcendentals=0, bytes_accessed=24 * count * rows * width
        ),
        name="gather_blocks",
    )(block)
    return whole.reshape(count, rows, width)


def on_device(
    kspace, coil_maps, sample_mask, tap_order, first_kernel, first_bias, second_kernel, second_bias
):
    position = lax.axis_index("slc")
    slab_depth = coil_maps.shape[1]
    slices = kspace.shape[1]
    points = kspace.shape[3]
    table_cols = make_table(W, -1.0)
    table_rows = make_table(H, -1.0)
    table_depth = make_table(slices, -1.0)
    inverse_cols = make_table(W, 1.0)
    inverse_rows = make_table(H, 1.0)
    inverse_depth = make_table(slices, 1.0)
    point_rows = (position * points + jnp.arange(points, dtype=jnp.int32)) // W
    row_picker = (point_rows[None, :] == jnp.arange(H, dtype=jnp.int32)[:, None]).astype(
        jnp.bfloat16
    )
    sampled = jnp.einsum(
        "zch,hp->zcp",
        sample_mask.astype(jnp.bfloat16),
        row_picker,
        preferred_element_type=jnp.float32,
    )
    count = slices // slab_depth
    own_rows = points // W
    measured = kspace.reshape(2, slices, C, own_rows, W).astype(jnp.float32)
    sampled = sampled.reshape(slices, C, own_rows, W)
    map_real = coil_maps[0]
    map_imag = coil_maps[1]

    def adjoint(residual, ready=None):
        depth_back = jnp.einsum(
            "pjcrx,pjqk->kqcrx", residual, inverse_depth, preferred_element_type=jnp.float32
        ).astype(jnp.bfloat16)
        slabs = lax.all_to_all(depth_back, "slc", split_axis=0, concat_axis=0, tiled=True)
        if ready is not None:
            slabs, ready = lax.optimization_barrier((slabs, ready))
        slabs = slabs.reshape(count, slab_depth, 2, C, own_rows, W)
        slabs = jnp.transpose(slabs, (2, 1, 3, 0, 4, 5)).reshape(2, slab_depth, C, H, W)
        upward = jnp.einsum(
            "pscjx,pjqk->qsckx", slabs, inverse_rows, preferred_element_type=jnp.float32
        ).astype(jnp.bfloat16)
        image_back = jnp.einsum(
            "pscyj,pjqk->qscyk", upward, inverse_cols, preferred_element_type=jnp.float32
        )
        real_sum = jnp.sum(map_real * image_back[0] + map_imag * image_back[1], axis=1)
        imag_sum = jnp.sum(map_real * image_back[1] - map_imag * image_back[0], axis=1)
        combined = jnp.stack([real_sum, imag_sum])
        return combined if ready is None else (combined, ready)

    def point_normal(before):
        image_real = before[0][:, None]
        image_imag = before[1][:, None]
        coil_image = jnp.stack(
            [
                map_real * image_real - map_imag * image_imag,
                map_real * image_imag + map_imag * image_real,
            ]
        ).astype(jnp.bfloat16)
        row_done = jnp.einsum(
            "pscyj,pjqk->qscyk", coil_image, table_cols, preferred_element_type=jnp.float32
        ).astype(jnp.bfloat16)
        plane = jnp.einsum(
            "pscjx,pjqk->qsckx", row_done, table_rows, preferred_element_type=jnp.float32
        ).astype(jnp.bfloat16)
        plane = plane.reshape(2, slab_depth, C, count, own_rows, W)
        plane = jnp.transpose(plane, (3, 1, 0, 2, 4, 5))
        pencil = lax.all_to_all(plane, "slc", split_axis=0, concat_axis=0, tiled=True)
        pencil = pencil.reshape(slices, 2, C, own_rows, W)
        spectrum = jnp.einsum(
            "jpcrx,pjqk->qkcrx", pencil, table_depth, preferred_element_type=jnp.float32
        )
        residual = (sampled[None] * (spectrum - measured)).astype(jnp.bfloat16)
        return adjoint(residual)

    def coil_update(before, base):
        own_coils = C // count
        maps = maps_by_coil.reshape(count, own_coils, 2, slab_depth, H, W)
        own_real, own_imag = maps[:, :, 0], maps[:, :, 1]
        block = jnp.transpose(before, (1, 0, 2, 3)).astype(jnp.bfloat16)
        image = gather_blocks(block.reshape(slab_depth * 2 * H, W), count)
        image = image.reshape(count, slab_depth, 2, H, W)
        image_real = image[:, None, :, 0].astype(jnp.float32)
        image_imag = image[:, None, :, 1].astype(jnp.float32)
        coil_image = jnp.stack(
            [
                own_real * image_real - own_imag * image_imag,
                own_real * image_imag + own_imag * image_real,
            ]
        ).astype(jnp.bfloat16)
        row_done = jnp.einsum(
            "pncsyj,pjqk->qncsyk", coil_image, table_cols, preferred_element_type=jnp.float32
        ).astype(jnp.bfloat16)
        plane = jnp.einsum(
            "pncsjx,pjqk->qncskx", row_done, table_rows, preferred_element_type=jnp.float32
        ).astype(jnp.bfloat16)
        spectrum = jnp.einsum(
            "pncsyx,pnsqk->qkcyx",
            plane,
            table_depth.reshape(2, count, slab_depth, 2, slices),
            preferred_element_type=jnp.float32,
        )
        residual = (own_mask[None, ..., None] * spectrum).astype(jnp.bfloat16)
        depth_back = jnp.einsum(
            "pjcyx,pjqns->qncsyx",
            residual,
            inverse_depth.reshape(2, slices, 2, count, slab_depth),
            preferred_element_type=jnp.float32,
        ).astype(jnp.bfloat16)
        upward = jnp.einsum(
            "pncsjx,pjqk->qncskx", depth_back, inverse_rows, preferred_element_type=jnp.float32
        ).astype(jnp.bfloat16)
        image_back = jnp.einsum(
            "pncsyj,pjqk->qncsyk", upward, inverse_cols, preferred_element_type=jnp.float32
        )
        real_sum = jnp.sum(own_real * image_back[0] + own_imag * image_back[1], axis=1)
        imag_sum = jnp.sum(own_real * image_back[1] - own_imag * image_back[0], axis=1)
        partial = jnp.stack([real_sum, imag_sum], axis=2).astype(jnp.bfloat16)
        base = jnp.transpose(base, (1, 0, 2, 3)).reshape(slab_depth * 2 * H, W)
        update, wide = sum_scatter(partial.reshape(count, slab_depth * 2 * H, W), base)
        update = jnp.transpose(update.reshape(slab_depth, 2, H, W), (1, 0, 2, 3))
        wide = wide.reshape(3 * slab_depth, 2, H, W)
        return update, wide[slab_depth - 2 : 2 * slab_depth + 2]

    kernel_one = tap_kernel(tap_order, first_kernel)
    kernel_two = tap_kernel(tap_order, second_kernel)
    global_slice = position * slab_depth - 1 + jnp.arange(slab_depth + 2, dtype=jnp.int32)
    inside = (global_slice >= 0) & (global_slice < slices)
    weights = denoiser_weights(
        slab_depth, kernel_one, first_bias, kernel_two, second_bias, inside
    )
    by_coil = C % count == 0 and count > 1 and count & (count - 1) == 0
    data = (sampled[None] * measured).astype(jnp.bfloat16)
    if by_coil:
        maps_by_coil = jnp.transpose(coil_maps, (2, 0, 1, 3, 4))
        maps_by_coil = lax.all_to_all(
            maps_by_coil, "slc", split_axis=0, concat_axis=0, tiled=True
        )
        own_mask = lax.dynamic_slice_in_dim(
            sample_mask, position * (C // count), C // count, axis=1
        ).astype(jnp.float32)
        ready = (own_mask, weights)
    else:
        ready = (weights,)
    estimate, ready = adjoint(data, ready)
    weights = ready[-1]
    if by_coil:
        own_mask = ready[0]
    before = estimate
    if by_coil:
        update, widened = coil_update(before, before + estimate)
    else:
        update = before - point_normal(before)
        field_low = update.astype(jnp.bfloat16)
        widened = jnp.transpose(padded_2(field_low, (("slc", 1),), 2), (1, 0, 2, 3))
    estimate = update - denoise(widened, *weights)
    dual_var = update - estimate
    return (estimate, dual_var)


def solution(mesh):
    placed = (
        P("grp", None, None, "slc"),
        P("grp", "slc", None, None, None),
        P("grp", None, None),
        P(),
        P(),
        P(),
        P(),
        P(),
    )
    return jax.shard_map(
        on_device,
        mesh=mesh,
        in_specs=placed,
        out_specs=(P("grp", "slc", None, None), P("grp", "slc", None, None)),
        check_vma=False,
    )
```

```python
import functools
import math

import jax
import jax.numpy as jnp
from jax import lax
from jax.experimental import pallas as pl
from jax.experimental.pallas import tpu as pltpu
from jax.sharding import PartitionSpec as P

C = 16
H = 128
W = 128


def padded_2(cells, sides, width):
    for axis, dim in sides:
        count = lax.axis_size(axis)
        ends = count - 1
        head = lax.slice_in_dim(cells, 0, width, axis=dim)
        tail = lax.slice_in_dim(cells, cells.shape[dim] - width, cells.shape[dim], axis=dim)
        cells = jnp.concatenate(
            [
                lax.ppermute(tail, axis, [(i, (i + 1) % count) for i in range(ends)]),
                cells,
                lax.ppermute(head, axis, [((i + 1) % count, i) for i in range(ends)]),
            ],
            axis=dim,
        )
    return cells


def make_table(length, direction):
    positions = jnp.arange(length, dtype=jnp.int32)
    product = positions[:, None] * positions[None, :] % length
    angles = 2.0 * math.pi / length * product.astype(jnp.float32)
    norm_scale = 1.0 / math.sqrt(length)
    real_part = (jnp.cos(angles) * norm_scale).astype(jnp.bfloat16)
    imaginary = (direction * jnp.sin(angles) * norm_scale).astype(jnp.bfloat16)
    real_t = jnp.transpose(real_part)
    imag_t = jnp.transpose(imaginary)
    upper = jnp.stack([real_t, imag_t], axis=1)
    lower = jnp.stack([-imag_t, real_t], axis=1)
    return jnp.stack([upper, lower])


def tap_kernel(tap_order, stored):
    chosen = (tap_order[None, :] == jnp.arange(27, dtype=jnp.int32)[:, None]).astype(jnp.bfloat16)
    return jnp.einsum("tq,qio->tio", chosen, stored, preferred_element_type=jnp.float32).astype(
        jnp.bfloat16
    )


def conv_kernel(
    depth, height, width, rows, columns_ref, one_ref, bias_ref, two_ref, out_bias_ref, noise_ref, terms
):
    block = rows * width
    group = noise_ref.shape[0]
    band = columns_ref.shape[0]
    lane = lax.broadcasted_iota(jnp.int32, (band, block + 2 * width), 1) % width
    out_lane = lax.broadcasted_iota(jnp.int32, (group, block), 1) % width
    terms[:, :width] = jnp.zeros((terms.shape[0], width), jnp.float32)
    terms[:, (height + 1) * width :] = jnp.zeros((terms.shape[0], width), jnp.float32)

    def hidden_step(step, carry):
        start = pl.multiple_of(step * block, block)
        here = columns_ref[:, pl.ds(start, block + 2 * width)]
        wide = here.astype(jnp.float32)
        span = block + 2 * width
        left = jnp.where(lane == 0, 0.0, pltpu.roll(wide, 1, 1)).astype(jnp.bfloat16)
        right = jnp.where(lane == width - 1, 0.0, pltpu.roll(wide, span - 1, 1))
        shifted = jnp.concatenate([left, here, right.astype(jnp.bfloat16)], axis=0)
        columns = jnp.concatenate(
            [shifted[:, row * width : row * width + block] for row in range(3)], axis=0
        )
        summed = jnp.dot(one_ref[...], columns, preferred_element_type=jnp.float32)
        hidden = jnp.maximum(summed + bias_ref[:, :1], 0.0)
        terms[:, pl.ds(pl.multiple_of(start + width, width), block)] = jnp.dot(
            two_ref[...], hidden.astype(jnp.bfloat16), preferred_element_type=jnp.float32
        )
        return carry

    lax.fori_loop(0, height // rows, hidden_step, 0)

    def sum_step(step, carry):
        start = pl.multiple_of(step * block, block)
        sums = []
        for column_shift in range(3):
            total = None
            for row_shift in range(3):
                first = (3 * row_shift + column_shift) * group
                piece = terms[
                    first : first + group,
                    pl.ds(pl.multiple_of(start + row_shift * width, width), block),
                ]
                total = piece if total is None else total + piece
            sums.append(total)
        left = jnp.where(out_lane == 0, 0.0, pltpu.roll(sums[0], 1, 1))
        right = jnp.where(out_lane == width - 1, 0.0, pltpu.roll(sums[2], block - 1, 1))
        noise_ref[:, pl.ds(start, block)] = left + sums[1] + right + out_bias_ref[:, :1]
        return carry

    lax.fori_loop(0, height // rows, sum_step, 0)


def denoiser_weights(depth, kernel_one, first_bias, kernel_two, second_bias, inside):
    channels, hid = kernel_one.shape[1:]
    deep = depth + 4
    mid = depth + 2
    band = -(-channels * deep // 16) * 16
    group = -(-channels * depth // 8) * 8
    taps = jnp.arange(3)
    place_one = (
        jnp.arange(deep)[None, :, None] == jnp.arange(mid)[:, None, None] + taps[None, None, :]
    ).astype(jnp.bfloat16)
    place_two = (
        jnp.arange(mid)[None, :, None] == jnp.arange(depth)[:, None, None] + taps[None, None, :]
    ).astype(jnp.bfloat16)
    one = jnp.einsum(
        "szd,dyxio->soyxzi",
        place_one,
        kernel_one.reshape(3, 3, 3, channels, hid),
        preferred_element_type=jnp.float32,
    ).astype(jnp.bfloat16)
    one = one.reshape(mid * hid, 9, deep * channels)
    one = jnp.pad(one, ((0, 0), (0, 0), (0, band - deep * channels))).reshape(mid * hid, 9 * band)
    two = jnp.einsum(
        "zsd,dyxho->yxozsh",
        place_two,
        kernel_two.reshape(3, 3, 3, hid, channels),
        preferred_element_type=jnp.float32,
    ).astype(jnp.bfloat16)
    two = two.reshape(9, depth * channels, mid * hid)
    two = two * jnp.repeat(inside.astype(jnp.bfloat16), hid)
    two = jnp.pad(two, ((0, 0), (0, group - depth * channels), (0, 0))).reshape(9 * group, mid * hid)
    bias = jnp.tile(first_bias, mid)[:, None]
    out_bias = jnp.pad(jnp.repeat(second_bias, depth), (0, group - depth * channels))[:, None]
    return one, bias, two, out_bias


def denoise(widened, one, bias, two, out_bias):
    deep, channels, height, width = widened.shape
    depth = deep - 4
    group = out_bias.shape[0]
    band = one.shape[1] // 9
    columns = widened.reshape(deep * channels, height * width)
    columns = jnp.pad(columns, ((0, band - deep * channels), (width, width)))
    rows = math.gcd(16, height)
    noise = pl.pallas_call(
        functools.partial(conv_kernel, depth, height, width, rows),
        out_shape=jax.ShapeDtypeStruct((group, height * width), jnp.float32),
        in_specs=[pl.BlockSpec(memory_space=pltpu.VMEM)] * 5,
        out_specs=pl.BlockSpec(memory_space=pltpu.VMEM),
        scratch_shapes=[pltpu.VMEM((9 * group, (height + 2) * width), jnp.float32)],
        compiler_params=pltpu.CompilerParams(vmem_limit_bytes=32 * 1024 * 1024),
        name="denoise",
    )(columns, one, bias, two, out_bias)
    return noise[: depth * channels].reshape(channels, depth, height, width)


def scatter_kernel(bits, partial_ref, base_ref, total_ref, wide_ref, *scratch):
    arrived, (send_sem, recv_sem, edge_send, edge_recv) = scratch[:-4], scratch[-4:]
    me = lax.axis_index("slc")
    mine = [me // 2**bit % 2 for bit in range(bits)]
    partner = [me + (1 - 2 * mine[bit]) * 2**bit for bit in range(bits)]
    half = partial_ref.shape[-2] // 2
    orders = [list(range(bits)), [0, *range(2, bits), 1][:bits]]

    count = 2**bits
    around = [(me + 1) % count, (me + count - 1) % count]

    barrier = pltpu.get_barrier_semaphore()
    for other in partner + around:
        pl.semaphore_signal(
            barrier, inc=1, device_id={"slc": other}, device_id_type=pl.DeviceIdType.MESH
        )
    pl.semaphore_wait(barrier, bits + 2)

    held = [partial_ref.at[..., pl.ds(chain * half, half), :] for chain in range(2)]
    left = [list(range(bits - 1, -1, -1)) for _ in range(2)]
    copies = [[], []]

    def part(chain, bit, choice):
        place = left[chain].index(bit)
        return held[chain].at[(slice(None),) * place + (choice,)]

    def send(chain, step):
        bit = orders[chain][step]
        copy = pltpu.make_async_remote_copy(
            src_ref=part(chain, bit, 1 - mine[bit]),
            dst_ref=arrived[chain * bits + step],
            send_sem=send_sem.at[chain, step],
            recv_sem=recv_sem.at[chain, step],
            device_id={"slc": partner[bit]},
            device_id_type=pl.DeviceIdType.MESH,
        )
        copy.start()
        copies[chain].append(copy)

    for chain in range(2):
        send(chain, 0)
    for step in range(bits):
        for chain in range(2):
            bit = orders[chain][step]
            landed = arrived[chain * bits + step]
            copies[chain][step].wait_recv()
            kept = part(chain, bit, mine[bit])[...].astype(jnp.float32)
            summed = kept + landed[...].astype(jnp.float32)
            if step == bits - 1:
                rows = slice(chain * half, (chain + 1) * half)
                update = base_ref[rows, :] - summed
                total_ref[rows, :] = update
                wide_ref[1, rows, :] = update.astype(wide_ref.dtype)
            else:
                landed[...] = summed.astype(landed.dtype)
                held[chain] = landed
                left[chain].remove(bit)
                send(chain, step + 1)
    edges = []
    for side in range(2):
        copy = pltpu.make_async_remote_copy(
            src_ref=wide_ref.at[1],
            dst_ref=wide_ref.at[2 * side],
            send_sem=edge_send.at[side],
            recv_sem=edge_recv.at[side],
            device_id={"slc": around[side]},
            device_id_type=pl.DeviceIdType.MESH,
        )
        copy.start()
        edges.append(copy)
    for chain in range(2):
        for copy in copies[chain]:
            copy.wait_send()
    for copy in edges:
        copy.wait_recv()
    for side, present in ((0, me > 0), (2, me < count - 1)):
        wide_ref[side] = wide_ref[side] * present.astype(jnp.float32).astype(wide_ref.dtype)
    for copy in edges:
        copy.wait_send()


def sum_scatter(partial, base):
    count, rows, width = partial.shape
    bits = count.bit_length() - 1
    landing = [
        pltpu.VMEM((2,) * (bits - 1 - step) + (rows // 2, width), partial.dtype)
        for _ in range(2)
        for step in range(bits)
    ]
    return pl.pallas_call(
        functools.partial(scatter_kernel, bits),
        out_shape=[
            jax.ShapeDtypeStruct((rows, width), jnp.float32),
            jax.ShapeDtypeStruct((3, rows, width), partial.dtype),
        ],
        in_specs=[pl.BlockSpec(memory_space=pltpu.VMEM)] * 2,
        out_specs=[pl.BlockSpec(memory_space=pltpu.VMEM)] * 2,
        scratch_shapes=landing
        + [pltpu.SemaphoreType.DMA((2, bits))] * 2
        + [pltpu.SemaphoreType.DMA((2,))] * 2,
        compiler_params=pltpu.CompilerParams(
            collective_id=0, has_side_effects=True, vmem_limit_bytes=32 * 1024 * 1024
        ),
        name="sum_scatter",
    )(partial.reshape((2,) * bits + (rows, width)), base)


def gather_kernel(bits, block_ref, whole_ref, send_sem, recv_sem):
    me = lax.axis_index("slc")
    mine = [me // 2**bit % 2 for bit in range(bits)]
    partner = [me + (1 - 2 * mine[bit]) * 2**bit for bit in range(bits)]
    half = block_ref.shape[0] // 2
    orders = [list(range(bits)), [0, *range(2, bits), 1][:bits]]

    barrier = pltpu.get_barrier_semaphore()
    for bit in range(bits):
        pl.semaphore_signal(
            barrier, inc=1, device_id={"slc": partner[bit]}, device_id_type=pl.DeviceIdType.MESH
        )
    whole_ref[tuple(mine[::-1])] = block_ref[...]
    pl.semaphore_wait(barrier, bits)

    copies = [[], []]
    for step in range(bits):
        for chain in range(2):
            order = orders[chain][::-1]
            if step:
                copies[chain][-1].wait_recv()
            place = tuple(
                slice(None) if bit in order[:step] else mine[bit]
                for bit in range(bits - 1, -1, -1)
            )
            held = whole_ref.at[place + (pl.ds(chain * half, half),)]
            copy = pltpu.make_async_remote_copy(
                src_ref=held,
                dst_ref=held,
                send_sem=send_sem.at[chain, step],
                recv_sem=recv_sem.at[chain, step],
                device_id={"slc": partner[order[step]]},
                device_id_type=pl.DeviceIdType.MESH,
            )
            copy.start()
            copies[chain].append(copy)
    for chain in range(2):
        copies[chain][-1].wait_recv()
    for chain in range(2):
        for copy in copies[chain]:
            copy.wait_send()


def gather_blocks(block, count):
    rows, width = block.shape
    bits = count.bit_length() - 1
    whole = pl.pallas_call(
        functools.partial(gather_kernel, bits),
        out_shape=jax.ShapeDtypeStruct((2,) * bits + (rows, width), block.dtype),
        in_specs=[pl.BlockSpec(memory_space=pltpu.VMEM)],
        out_specs=pl.BlockSpec(memory_space=pltpu.VMEM),
        scratch_shapes=[pltpu.SemaphoreType.DMA((2, bits)), pltpu.SemaphoreType.DMA((2, bits))],
        compiler_params=pltpu.CompilerParams(
            collective_id=1, has_side_effects=True, vmem_limit_bytes=32 * 1024 * 1024
        ),
        cost_estimate=pl.CostEstimate(
            flops=0, transcendentals=0, bytes_accessed=24 * count * rows * width
        ),
        name="gather_blocks",
    )(block)
    return whole.reshape(count, rows, width)


def on_device(
    kspace, coil_maps, sample_mask, tap_order, first_kernel, first_bias, second_kernel, second_bias
):
    position = lax.axis_index("slc")
    slab_depth = coil_maps.shape[1]
    slices = kspace.shape[1]
    points = kspace.shape[3]
    table_cols = make_table(W, -1.0)
    table_rows = make_table(H, -1.0)
    table_depth = make_table(slices, -1.0)
    inverse_cols = make_table(W, 1.0)
    inverse_rows = make_table(H, 1.0)
    inverse_depth = make_table(slices, 1.0)
    point_rows = (position * points + jnp.arange(points, dtype=jnp.int32)) // W
    row_picker = (point_rows[None, :] == jnp.arange(H, dtype=jnp.int32)[:, None]).astype(
        jnp.bfloat16
    )
    sampled = jnp.einsum(
        "zch,hp->zcp",
        sample_mask.astype(jnp.bfloat16),
        row_picker,
        preferred_element_type=jnp.float32,
    )
    count = slices // slab_depth
    own_rows = points // W
    measured = kspace.reshape(2, slices, C, own_rows, W).astype(jnp.float32)
    sampled = sampled.reshape(slices, C, own_rows, W)
    map_real = coil_maps[0]
    map_imag = coil_maps[1]

    def adjoint(residual, ready=None):
        depth_back = jnp.einsum(
            "pjcrx,pjqk->kqcrx", residual, inverse_depth, preferred_element_type=jnp.float32
        ).astype(jnp.bfloat16)
        slabs = lax.all_to_all(depth_back, "slc", split_axis=0, concat_axis=0, tiled=True)
        if ready is not None:
            slabs, ready = lax.optimization_barrier((slabs, ready))
        slabs = slabs.reshape(count, slab_depth, 2, C, own_rows, W)
        slabs = jnp.transpose(slabs, (2, 1, 3, 0, 4, 5)).reshape(2, slab_depth, C, H, W)
        upward = jnp.einsum(
            "pscjx,pjqk->qsckx", slabs, inverse_rows, preferred_element_type=jnp.float32
        ).astype(jnp.bfloat16)
        image_back = jnp.einsum(
            "pscyj,pjqk->qscyk", upward, inverse_cols, preferred_element_type=jnp.float32
        )
        real_sum = jnp.sum(map_real * image_back[0] + map_imag * image_back[1], axis=1)
        imag_sum = jnp.sum(map_real * image_back[1] - map_imag * image_back[0], axis=1)
        combined = jnp.stack([real_sum, imag_sum])
        return combined if ready is None else (combined, ready)

    def point_normal(before):
        image_real = before[0][:, None]
        image_imag = before[1][:, None]
        coil_image = jnp.stack(
            [
                map_real * image_real - map_imag * image_imag,
                map_real * image_imag + map_imag * image_real,
            ]
        ).astype(jnp.bfloat16)
        row_done = jnp.einsum(
            "pscyj,pjqk->qscyk", coil_image, table_cols, preferred_element_type=jnp.float32
        ).astype(jnp.bfloat16)
        plane = jnp.einsum(
            "pscjx,pjqk->qsckx", row_done, table_rows, preferred_element_type=jnp.float32
        ).astype(jnp.bfloat16)
        plane = plane.reshape(2, slab_depth, C, count, own_rows, W)
        plane = jnp.transpose(plane, (3, 1, 0, 2, 4, 5))
        pencil = lax.all_to_all(plane, "slc", split_axis=0, concat_axis=0, tiled=True)
        pencil = pencil.reshape(slices, 2, C, own_rows, W)
        spectrum = jnp.einsum(
            "jpcrx,pjqk->qkcrx", pencil, table_depth, preferred_element_type=jnp.float32
        )
        residual = (sampled[None] * (spectrum - measured)).astype(jnp.bfloat16)
        return adjoint(residual)

    def coil_update(before, base):
        own_coils = C // count
        maps = maps_by_coil.reshape(count, own_coils, 2, slab_depth, H, W)
        own_real, own_imag = maps[:, :, 0], maps[:, :, 1]
        block = before.astype(jnp.bfloat16).reshape(2 * slab_depth * H, W)
        image = gather_blocks(block, count).reshape(count, 2, slab_depth, H, W)
        image_real = image[:, None, 0].astype(jnp.float32)
        image_imag = image[:, None, 1].astype(jnp.float32)
        coil_image = jnp.stack(
            [
                own_real * image_real - own_imag * image_imag,
                own_real * image_imag + own_imag * image_real,
            ]
        ).astype(jnp.bfloat16)
        row_done = jnp.einsum(
            "pncsyj,pjqk->qncsyk", coil_image, table_cols, preferred_element_type=jnp.float32
        ).astype(jnp.bfloat16)
        plane = jnp.einsum(
            "pncsjx,pjqk->qncskx", row_done, table_rows, preferred_element_type=jnp.float32
        ).astype(jnp.bfloat16)
        spectrum = jnp.einsum(
            "pncsyx,pnsqk->qkcyx",
            plane,
            table_depth.reshape(2, count, slab_depth, 2, slices),
            preferred_element_type=jnp.float32,
        )
        residual = (own_mask[None, ..., None] * spectrum).astype(jnp.bfloat16)
        depth_back = jnp.einsum(
            "pjcyx,pjqns->qncsyx",
            residual,
            inverse_depth.reshape(2, slices, 2, count, slab_depth),
            preferred_element_type=jnp.float32,
        ).astype(jnp.bfloat16)
        upward = jnp.einsum(
            "pncsjx,pjqk->qncskx", depth_back, inverse_rows, preferred_element_type=jnp.float32
        ).astype(jnp.bfloat16)
        image_back = jnp.einsum(
            "pncsyj,pjqk->qncsyk", upward, inverse_cols, preferred_element_type=jnp.float32
        )
        real_sum = jnp.sum(own_real * image_back[0] + own_imag * image_back[1], axis=1)
        imag_sum = jnp.sum(own_real * image_back[1] - own_imag * image_back[0], axis=1)
        partial = jnp.stack([real_sum, imag_sum], axis=1).astype(jnp.bfloat16)
        base = base.reshape(2 * slab_depth * H, W)
        update, wide = sum_scatter(partial.reshape(count, slab_depth * 2 * H, W), base)
        update = update.reshape(2, slab_depth, H, W)
        wide = jnp.transpose(wide.reshape(3, 2, slab_depth, H, W), (0, 2, 1, 3, 4))
        wide = wide.reshape(3 * slab_depth, 2, H, W)
        return update, wide[slab_depth - 2 : 2 * slab_depth + 2]

    kernel_one = tap_kernel(tap_order, first_kernel)
    kernel_two = tap_kernel(tap_order, second_kernel)
    global_slice = position * slab_depth - 1 + jnp.arange(slab_depth + 2, dtype=jnp.int32)
    inside = (global_slice >= 0) & (global_slice < slices)
    weights = denoiser_weights(
        slab_depth, kernel_one, first_bias, kernel_two, second_bias, inside
    )
    by_coil = C % count == 0 and count > 1 and count & (count - 1) == 0
    data = (sampled[None] * measured).astype(jnp.bfloat16)
    if by_coil:
        maps_by_coil = jnp.transpose(coil_maps, (2, 0, 1, 3, 4))
        maps_by_coil = lax.all_to_all(
            maps_by_coil, "slc", split_axis=0, concat_axis=0, tiled=True
        )
        own_mask = lax.dynamic_slice_in_dim(
            sample_mask, position * (C // count), C // count, axis=1
        ).astype(jnp.float32)
        ready = (own_mask, weights)
    else:
        ready = (weights,)
    estimate, ready = adjoint(data, ready)
    weights = ready[-1]
    if by_coil:
        own_mask = ready[0]
    before = estimate
    if by_coil:
        update, widened = coil_update(before, before + estimate)
    else:
        update = before - point_normal(before)
        field_low = update.astype(jnp.bfloat16)
        widened = jnp.transpose(padded_2(field_low, (("slc", 1),), 2), (1, 0, 2, 3))
    estimate = update - denoise(widened, *weights)
    dual_var = update - estimate
    return (estimate, dual_var)


def solution(mesh):
    placed = (
        P("grp", None, None, "slc"),
        P("grp", "slc", None, None, None),
        P("grp", None, None),
        P(),
        P(),
        P(),
        P(),
        P(),
    )
    return jax.shard_map(
        on_device,
        mesh=mesh,
        in_specs=placed,
        out_specs=(P("grp", "slc", None, None), P("grp", "slc", None, None)),
        check_vma=False,
    )
```
